512 devices in a mesh: gz: 64 (over y, x, core), gy: 8 (over z).
Axes of the slice: x: 4, y: 8, z: 8, core: 2. Of those that a mesh axis runs over, the one named last changes fastest.
Arguments:
- log_kappa: float32 [128, 128, 128], P('gz', 'gy'), may hold values from -4 to 4
- misfit_weight: float32 [128, 128, 128], P('gz', 'gy'), may hold values from 0.25 to 2.5
- right_side: float32 [128, 128, 128], P('gz', 'gy'), may hold values from -72 to 72
- lift_gain: float32 [64], replicated, may hold values from -4 to 4
- lift_bias: float32 [64], replicated, may hold values from -3 to 3
- spec_one: float32 [128, 8, 32, 4096], P('gz', 'gy'), may hold values from -1.5 to 1.5
- spec_two: float32 [128, 8, 32, 4096], P('gz', 'gy'), may hold values from -1.5 to 1.5
- local_one: float32 [64, 64], replicated, may hold values from -0.75 to 0.75
- local_two: float32 [64, 64], replicated, may hold values from -0.75 to 0.75
- bias_one: float32 [64], replicated, may hold values from -3 to 3
- bias_two: float32 [64], replicated, may hold values from -3 to 3
- readout: float32 [64], replicated, may hold values from -0.75 to 0.75
Outputs:
- solution: float32 [128, 128, 128], P('gz', 'gy')
- residual: float32 [128, 128, 128], P('gz', 'gy')
The draws below stay inside these ranges and needn't reach their ends.
All inputs are finite; a program needn't handle non-finite values.
Results may differ from the reference program's by a relative error of at most 0.0017.
Values sent between devices are 32-bit elements; how exact they have to be, the bound alone decides.
A program may use at most 64 MiB of HBM per device.

```python
import math
import jax
import jax.numpy as jnp
from jax import lax

C = 64
KX = 32
KY = 32
KZ = 32
NX = 128
ITERS = 2
KXY = 128
CC = 4096
NY = 128
NZ = 128
N_GY = 8


def draw_right_side(key, part):
    key = jax.random.fold_in(key, 17)
    base_key, row_key, col_key = jax.random.split(key, 3)
    base = jnp.clip(jax.random.normal(base_key, (NZ, NY, NX), jnp.float32), -4.0, 4.0)
    row_scale = jnp.exp(jax.random.uniform(row_key, (NZ, NY, 1), jnp.float32, math.log(0.3), math.log(3.0)))
    col_scale = jnp.exp(jax.random.uniform(col_key, (1, 1, NX), jnp.float32, math.log(0.5), math.log(2.0)))
    ramp = jnp.exp(jnp.arange(NZ, dtype=jnp.float32)[:, None, None] * (math.log(3.0) / NZ))
    return base * row_scale * col_scale * ramp


def block_levels(key, extent, shards, smallest, top_value):
    level = 1.0
    for dim, shards_of in shards:
        steps = jax.random.uniform(jax.random.fold_in(jax.random.fold_in(key, 6), dim), (shards_of,), jnp.float32, smallest / len(shards), top_value / len(shards))
        level = level * jnp.repeat(jnp.exp(steps), extent[dim] // shards_of).reshape((-1,) + (1,) * (len(extent) - 1 - dim))
    return level


def noise(key, shape, width, reach, cuts=(), kind=jnp.bfloat16):
    drawn = jax.random.normal(key, shape, jnp.float32) * width
    if len(cuts) > 0:
        drawn = block_levels(key, shape, cuts, -0.22, 0.18) * drawn
    return jnp.clip(drawn, min=-reach, max=reach).astype(kind)


def setup_inputs(seed: int = 0) -> dict:
    arg_keys = jax.random.split(jax.random.key(seed), 13)
    return {
        "log_kappa": noise(arg_keys[0], (NZ, NY, NX), 1.0, 4.0, ((0, 64), (1, 8)), jnp.float32),
        "misfit_weight": jnp.clip(jnp.exp(math.log(2.5) - 2.3025851 * jax.random.uniform(arg_keys[1], (NZ, NY, NX), jnp.float32) ** block_levels(arg_keys[1], (NZ, NY, NX), ((0, 64), (1, 8)), -0.2, 0.2)), 0.25, 2.5),
        "right_side": draw_right_side(jax.random.fold_in(arg_keys[12], 71), 0),
        "lift_gain": noise(arg_keys[3], (C,), 1.0, 4.0, (), jnp.float32),
        "lift_bias": noise(arg_keys[4], (C,), 0.5, 3.0, (), jnp.float32),
        "spec_one": noise(arg_keys[5], (KXY, N_GY, KZ, CC), (C // 4) ** -0.5, 1.5, ((0, 64), (1, 8)), jnp.float32),
        "spec_two": noise(arg_keys[6], (KXY, N_GY, KZ, CC), (C // 4) ** -0.5, 1.5, ((0, 64), (1, 8)), jnp.float32),
        "local_one": noise(arg_keys[7], (C, C), C ** -0.5, 0.75, (), jnp.float32),
        "local_two": noise(arg_keys[8], (C, C), C ** -0.5, 0.75, (), jnp.float32),
        "bias_one": noise(arg_keys[9], (C,), 0.5, 3.0, (), jnp.float32),
        "bias_two": noise(arg_keys[10], (C,), 0.5, 3.0, (), jnp.float32),
        "readout": noise(arg_keys[11], (C,), C ** -0.5, 0.75, (), jnp.float32),
    }


HIGHEST = lax.Precision.HIGHEST
DAMPING = 0.3

def basis_table(modes, length):
    mode_index = jnp.arange(modes, dtype=jnp.int32)
    cell_index = jnp.arange(length, dtype=jnp.int32)
    frequency = (mode_index + 1) // 2
    phase_steps = frequency[:, None] * cell_index[None, :] % length
    angles = phase_steps.astype(jnp.float32) * (2.0 * math.pi / length)
    is_sine = (mode_index % 2 == 0) & (mode_index > 0)
    scales = jnp.where(mode_index == 0, math.sqrt(1.0 / length), math.sqrt(2.0 / length)).astype(jnp.float32)
    return jnp.where(is_sine[:, None], jnp.sin(angles), jnp.cos(angles)) * scales[:, None]

def gelu_parts(grid_field):
    normal_cdf = 0.5 * (1.0 + lax.erf(grid_field * (1.0 / math.sqrt(2.0))))
    density = jnp.exp(-0.5 * grid_field * grid_field) * (1.0 / math.sqrt(2.0 * math.pi))
    return (grid_field * normal_cdf, normal_cdf + grid_field * density)

def spectral(grid_field, weights, adjoint):
    table_x = basis_table(KX, NX)
    table_y = basis_table(KY, NY)
    table_z = basis_table(KZ, NZ)
    channels = grid_field.shape[0]
    coeffs = jnp.einsum('czyx,kx->czyk', grid_field, table_x, precision=HIGHEST)
    coeffs = jnp.einsum('czyk,jy->czjk', coeffs, table_y, precision=HIGHEST)
    coeffs = jnp.einsum('czjk,mz->cmjk', coeffs, table_z, precision=HIGHEST)
    coeffs = coeffs.reshape(channels, KZ, KY, KX // N_GY, N_GY)
    matrices = weights.reshape(KY, KX // N_GY, N_GY, KZ, channels, channels)
    if adjoint:
        coeffs = jnp.einsum('omjab,jabmio->imjab', coeffs, matrices, precision=HIGHEST)
    else:
        coeffs = jnp.einsum('imjab,jabmio->omjab', coeffs, matrices, precision=HIGHEST)
    coeffs = coeffs.reshape(channels, KZ, KY, KX)
    coeffs = jnp.einsum('cmjk,mz->czjk', coeffs, table_z, precision=HIGHEST)
    coeffs = jnp.einsum('czjk,jy->czyk', coeffs, table_y, precision=HIGHEST)
    return jnp.einsum('czyk,kx->czyx', coeffs, table_x, precision=HIGHEST)

def expand(vector):
    return vector[:, None, None, None]

def local_mix(matrix, grid_field):
    return jnp.einsum('io,izyx->ozyx', matrix, grid_field, precision=HIGHEST)

def local_back(matrix, grid_field):
    return jnp.einsum('io,ozyx->izyx', matrix, grid_field, precision=HIGHEST)

def reference(log_kappa, misfit_weight, right_side, lift_gain, lift_bias, spec_one, spec_two, local_one, local_two, bias_one, bias_two, readout):
    lifted = expand(lift_gain) * log_kappa[None] + expand(lift_bias)
    pre_one = spectral(lifted, spec_one, False) + local_mix(local_one, lifted) + expand(bias_one)
    act_one, slope_one = gelu_parts(pre_one)
    pre_two = spectral(act_one, spec_two, False) + local_mix(local_two, act_one) + expand(bias_two)
    unused_act, slope_two = gelu_parts(pre_two)

    def hessian(vector):
        lifted_dir = expand(lift_gain) * vector[None]
        tangent_one = slope_one * (spectral(lifted_dir, spec_one, False) + local_mix(local_one, lifted_dir))
        tangent_two = slope_two * (spectral(tangent_one, spec_two, False) + local_mix(local_two, tangent_one))
        predicted = jnp.einsum('c,czyx->zyx', readout, tangent_two, precision=HIGHEST)
        weighted = misfit_weight * predicted
        back_two = slope_two * (expand(readout) * weighted[None])
        back_one = slope_one * (spectral(back_two, spec_two, True) + local_back(local_two, back_two))
        grad_zero = spectral(back_one, spec_one, True) + local_back(local_one, back_one)
        return jnp.einsum('c,czyx->zyx', lift_gain, grad_zero, precision=HIGHEST) + DAMPING * vector
    solution = jnp.zeros_like(right_side)
    residual = right_side
    direction = right_side
    norm_now = jnp.sum(residual * residual)
    for iteration in range(ITERS):
        applied = hessian(direction)
        step_size = norm_now / jnp.sum(direction * applied)
        solution = solution + step_size * direction
        residual = residual - step_size * applied
        norm_next = jnp.sum(residual * residual)
        direction = residual + norm_next / norm_now * direction
        norm_now = norm_next
    return (solution, residual)
```

```python
import functools
import math

import jax
import jax.numpy as jnp
import ml_dtypes
import numpy as np
from jax import lax
from jax.experimental import pallas as pl
from jax.experimental.pallas import tpu as pltpu
from jax.sharding import PartitionSpec as P

KX = 32
KY = 32
KZ = 32
DAMPING = 0.3
HIGHEST = lax.Precision.HIGHEST
MESH = pl.DeviceIdType.MESH
NT = (((1,), (1,)), ((), ()))
UNITS = 15
B0K, B0R, C0A, C0T, D0A, D0T, E0, F0, G0, B1, C1, D1, E1, F1, G1 = range(UNITS)
SUMS = {E0: 0, C1: 1, E1: 2}
UNROLL = 2


def basis_table(modes, length):
    mode_index = np.arange(modes)
    frequency = (mode_index + 1) // 2
    phase_steps = frequency[:, None] * np.arange(length)[None, :] % length
    angles = phase_steps * (2.0 * math.pi / length)
    is_sine = (mode_index % 2 == 0) & (mode_index > 0)
    scales = np.where(mode_index == 0, math.sqrt(1.0 / length), math.sqrt(2.0 / length))
    return (np.where(is_sine[:, None], np.sin(angles), np.cos(angles)) * scales[:, None]).astype(np.float32)


def parts_of(table):
    high = table.astype(ml_dtypes.bfloat16)
    low = (table - high.astype(np.float32)).astype(ml_dtypes.bfloat16)
    return high, low


def wide(table):
    high, low = parts_of(table)
    return np.concatenate([high, low, high], axis=1)


class Sizes:
    def __init__(self, gz, gy, rows, line, kx, ky, kz):
        self.gz, self.gy, self.rows, self.line = gz, gy, rows, line
        self.kx, self.ky, self.kz = kx, ky, kz
        self.kxhi = kx // gy
        self.modes = ky * self.kxhi // gz * kz


def tables_of(s):
    bx, by, bz = basis_table(s.kx, s.line), basis_table(s.ky, s.rows * s.gy), basis_table(s.kz, 2 * s.gz)
    order = np.arange(s.kx).reshape(s.kxhi, s.gy).T.reshape(-1)
    tx = bx[order]
    eye = np.eye(s.kxhi, dtype=np.float32)
    ty = np.einsum("kY,ab->kabY", by, eye).reshape(s.ky * s.kxhi, s.kxhi * s.rows * s.gy)
    byd = by.reshape(s.ky, s.gy, s.rows)
    tyt = np.einsum("kdy,ab->dayKb".replace("K", "k"), byd, eye).reshape(s.gy * s.kxhi * s.rows, s.ky * s.kxhi)
    bzg = bz.reshape(s.kz, s.gz, 2)
    two = np.eye(2, dtype=np.float32)
    tz = np.einsum("kgz,ij->izkgj", bzg, two).reshape(4 * s.kz, 2 * s.gz)
    tza = np.einsum("kgz,ij->izkgj", bzg, np.eye(2, 4, dtype=np.float32)).reshape(4 * s.kz, 4 * s.gz)
    ma = np.zeros((s.gy, 2, 2, s.rows, s.ky, 2, 2), np.float32)
    for f in range(2):
        for z in range(2):
            ma[:, f, z, :, :, z, f] = byd.transpose(1, 2, 0)
    ma = ma.reshape(s.gy, 4 * s.rows, 4 * s.ky)
    full = np.zeros((s.gy, 128, 128), np.float32)
    full[:, : 4 * s.rows, : 4 * s.ky] = ma
    ym = np.broadcast_to(byd.transpose(1, 0, 2)[:, :, None, None, None, :], (s.gy, s.ky, s.kxhi, s.kxhi, 2, s.rows))
    ym = np.ascontiguousarray(ym).reshape(s.gy, s.ky * s.kxhi, s.kxhi * 2 * s.rows)
    lanes = np.arange(128)
    expand = (np.arange(128)[None, :, None] % 64 == 2 * np.arange(32)[:, None, None] + lanes[None, None, :] // 64)
    return [
        tx,
        bx.reshape(s.kxhi, s.gy, s.line),
        wide(tx),
        wide(np.ascontiguousarray(tx.T)),
        wide(ty),
        wide(tyt),
        wide(tz),
        wide(np.ascontiguousarray(tz.T)),
        tza,
        full,
        ym,
        expand.astype(ml_dtypes.bfloat16),
    ]


def split(x):
    high = x.astype(jnp.bfloat16)
    return high, (x - high.astype(jnp.float32)).astype(jnp.bfloat16)


def tall3(x):
    high, low = split(x)
    return jnp.concatenate([high, high, low], axis=0)


def flat3(x):
    high, low = split(x)
    return jnp.concatenate([high, high, low], axis=1)


def dot(a, b):
    return jnp.dot(a, b, preferred_element_type=jnp.float32)


def gelu_parts(grid_field):
    normal_cdf = 0.5 * (1.0 + lax.erf(grid_field * (1.0 / math.sqrt(2.0))))
    density = jnp.exp(-0.5 * grid_field * grid_field) * (1.0 / math.sqrt(2.0 * math.pi))
    return (grid_field * normal_cdf, normal_cdf + grid_field * density)


def total(x):
    return jnp.sum(jnp.sum(x, axis=0, keepdims=True), axis=1, keepdims=True)


def kernel(s, *refs):
    (kappa, weight, rhs, vec, gexp, w1, w2, mats,
     tx, txk, tx3, txt3, ty3, tyt3, tz3, tzt3, tza, ma, ym, expand,
     out_solution, out_residual,
     send_y, recv_y, send_z, recv_z, send_zs, recv_zs, send_s, recv_s,
     send_a, recv_a, send_az, recv_az, send_pz, recv_pz, send_py, recv_py,
     mats3, kb, rb, wb, slope_one, slope_two, act, tan, back, pred0, qb, lb,
     sy, ry, sz, rz, ss, rs, sa, ra, spz, rpz, spy, rpy) = refs
    me_z, me_y = lax.axis_index("gz"), lax.axis_index("gy")
    core, chip = lax.rem(me_z, 2), lax.div(me_z, 2)
    chunk = s.kxhi * s.rows
    f32 = jnp.float32

    barrier = pltpu.get_barrier_semaphore()
    for k in range(1, s.gy):
        pl.semaphore_signal(barrier, inc=1, device_id={"gy": lax.rem(me_y + k, s.gy)}, device_id_type=MESH)

    def greet(k, carry):
        pl.semaphore_signal(barrier, inc=1, device_id={"gz": lax.rem(me_z + k, s.gz)}, device_id_type=MESH)
        return carry

    lax.fori_loop(1, s.gz, greet, 0)
    pl.semaphore_wait(barrier, s.gy + s.gz - 2)

    hops = sorted(range(1, s.gy), key=lambda k: -min(k, s.gy - k))

    def exchange_gy(src_of, dst, send_sem, recv_sem):
        for k in hops:
            peer = lax.rem(me_y + k, s.gy)
            pltpu.make_async_remote_copy(
                src_of(peer), dst, send_sem, recv_sem, device_id={"gy": peer}, device_id_type=MESH
            ).start()
        pltpu.make_async_copy(src_of(me_y), dst, recv_sem).start()

    def exchange_gz(src_of, dst, send_sem, recv_sem):
        def step(k, carry):
            peer = lax.rem(me_z + k, s.gz)
            pltpu.make_async_remote_copy(
                src_of(peer), dst, send_sem, recv_sem, device_id={"gz": peer}, device_id_type=MESH
            ).start()
            return carry

        lax.fori_loop(1, s.gz, step, 0)
        pltpu.make_async_copy(src_of(me_z), dst, recv_sem).start()

    def wait(ref, sem):
        pltpu.make_async_copy(ref, ref, sem).wait()

    def unit_gy(e):
        exchange_gy(
            lambda p: send_y.at[e, pl.ds(pl.multiple_of(p * chunk, chunk), chunk)],
            recv_y.at[e, pl.ds(pl.multiple_of(me_y * chunk, chunk), chunk)],
            sy.at[e], ry.at[e],
        )

    def wait_gy(e):
        wait(recv_y.at[e], ry.at[e])

    def unit_gz(e):
        if e in SUMS:
            i = SUMS[e]
            exchange_gz(lambda p: send_zs.at[i, p], recv_zs.at[i, me_z], sz.at[e], rz.at[e])
        else:
            exchange_gz(lambda p: send_z.at[e, p], recv_z.at[e, me_z], sz.at[e], rz.at[e])

    def wait_gz(e):
        if e in SUMS:
            wait(recv_zs.at[SUMS[e]], rz.at[e])
        else:
            wait(recv_z.at[e], rz.at[e])

    lane = lax.broadcasted_iota(jnp.int32, (1, 128), 1)
    low_half = (lane < 64).astype(f32)
    high_half = 1.0 - low_half

    both = jnp.concatenate([kappa[...], rhs[...], jnp.zeros((128 - 4 * s.rows, 128), f32)], axis=0)
    spectrum = lax.dot_general(tx[...], both, NT, precision=HIGHEST, preferred_element_type=f32)
    own = jnp.sum(rhs[...] * rhs[...], axis=0, keepdims=True)
    send_a[...] = jnp.zeros_like(send_a)
    for h in range(s.gy):
        send_a[h, 0 : s.kxhi, :] = spectrum[h * s.kxhi : (h + 1) * s.kxhi]
        send_a[h, s.kxhi : s.kxhi + 1, :] = own
    exchange_gy(lambda p: send_a.at[p], recv_a.at[me_y], sa.at[0], ra.at[0])

    for m in range(mats.shape[0]):
        high, low = split(mats[m])
        mats3[m, 0:128, :] = high
        mats3[m, 128:256, :] = low
        mats3[m, 256:384, :] = high
    mix_two, mix_back, read_mat, lift_mat = range(4)

    gain_mix = jnp.zeros((s.modes, 128), f32)
    bias_mix = jnp.zeros((8, 128), f32)
    for t in range(32):
        gain_mix = gain_mix + w1[:, t * 128 : (t + 1) * 128] * gexp[0:1, t * 128 : (t + 1) * 128]
        bias_mix = bias_mix + w1[0:8, t * 128 : (t + 1) * 128] * gexp[1:2, t * 128 : (t + 1) * 128]
    gain_mix = gain_mix + pltpu.roll(gain_mix, 64, 1)
    bias_mix = bias_mix + pltpu.roll(bias_mix, 64, 1)
    is_mean = ((me_z == 0) & (me_y == 0)).astype(f32)
    first_row = (lax.broadcasted_iota(jnp.int32, (8, 128), 0) == 0).astype(f32)
    volume = math.sqrt(float(2 * s.gz) * float(s.rows * s.gy) * float(s.line))
    bias_mix = bias_mix * first_row * (is_mean * volume)

    wait(recv_a, ra.at[0])
    mixed = jnp.zeros((8, 128), f32)
    own = jnp.zeros((1, 128), f32)
    for d in range(s.gy):
        mixed = mixed + jnp.dot(recv_a[d], ma[d], precision=HIGHEST, preferred_element_type=f32)
        own = own + recv_a[d, s.kxhi : s.kxhi + 1, :]
    for c in range(2):
        send_az[c, 0:2, :] = mixed[2 * c : 2 * c + 2]
        send_az[c, 2:3, :] = own
        send_az[c, 3:4, :] = jnp.zeros((1, 128), f32)
    exchange_gz(lambda p: send_az.at[lax.rem(p, 2)], recv_az.at[me_z], sa.at[1], ra.at[1])

    def spread(y, carry):
        for src, dst in ((kappa, kb), (rhs, rb), (weight, wb)):
            near = jnp.broadcast_to(src[pl.ds(y, 1), :], (64, 128))
            far = jnp.broadcast_to(src[pl.ds(s.rows + y, 1), :], (64, 128))
            dst[y] = jnp.concatenate([near, far], axis=0).T
        return carry

    lax.fori_loop(0, s.rows, spread, 0)

    wait(recv_az, ra.at[1])
    arrived = recv_az[...].reshape(4 * s.gz, 128)
    row = lax.broadcasted_iota(jnp.int32, (4 * s.gz, 128), 0)
    norm_zero = total(jnp.where(lax.rem(row, 4) == 2, arrived, 0.0))
    coeffs = jnp.dot(tza[...], arrived, precision=HIGHEST, preferred_element_type=f32)

    def pick(f):
        columns = []
        for j in range(2):
            kept = jnp.zeros((s.kz, 128), f32)
            for z in range(2):
                at = (2 * j + z) * s.kz
                kept = kept + coeffs[at : at + s.kz] * (lane == chip * 4 + z * 2 + f).astype(f32)
            columns.append(jnp.sum(kept, axis=1, keepdims=True))
        return jnp.concatenate(columns, axis=0)

    modes_kappa, modes_rhs = pick(0), pick(1)

    def cells_z(e, values):
        pieces = []
        for j in range(2):
            half = values[j * s.kz : (j + 1) * s.kz]
            pieces += [half * low_half, half * high_half]
        sent = dot(tzt3[...], tall3(jnp.concatenate(pieces, axis=0)))
        send_z[e] = sent.reshape(s.gz, 2, 128)
        unit_gz(e)

    def cells_y(e):
        wait_gz(e)
        send_y[e] = dot(tyt3[...], tall3(recv_z[e].reshape(2 * s.gz, 128)))
        unit_gy(e)

    def cells_x(e, y):
        return dot(txt3[...], tall3(recv_y[e, pl.ds(y, s.kx, stride=s.rows), :]))

    def modes_x(e, y, field):
        send_y[e, pl.ds(y, s.kx, stride=s.rows), :] = dot(tx3[...], tall3(field))

    def modes_sum(e, partial):
        i = SUMS[e]
        send_s[i] = jnp.broadcast_to(partial, (8, 128))
        exchange_gy(lambda p: send_s.at[i], recv_s.at[i, me_y], ss.at[i], rs.at[i])

    def modes_y(e):
        wait_gy(e)
        highs, lows = [], []
        for a in range(s.kxhi):
            for d in range(s.gy):
                at = d * chunk + a * s.rows
                high, low = split(recv_y[e, at : at + s.rows, :])
                highs.append(high)
                lows.append(low)
        sent = dot(ty3[...], jnp.concatenate(highs + highs + lows, axis=0)).reshape(s.gz, 2, 128)
        if e in SUMS:
            i = SUMS[e]
            wait(recv_s.at[i], rs.at[i])
            partial = jnp.zeros((1, 128), f32)
            for d in range(s.gy):
                partial = partial + recv_s[i, d, 0:1, :]
            send_zs[i, :, 0:2, :] = sent
            send_zs[i, :, 2:4, :] = jnp.broadcast_to(partial[None], (s.gz, 2, 128))
        else:
            send_z[e] = sent
        unit_gz(e)

    def modes_z(e):
        wait_gz(e)
        summed = None
        if e in SUMS:
            i = SUMS[e]
            arrived = recv_zs[i, :, 0:2, :].reshape(2 * s.gz, 128)
            summed = total(recv_zs[i, :, 2:3, :].reshape(s.gz, 128))
        else:
            arrived = recv_z[e].reshape(2 * s.gz, 128)
        coeffs = dot(tz3[...], tall3(arrived))
        pieces = []
        for j in range(2):
            at = 2 * j * s.kz
            pieces.append(coeffs[at : at + s.kz] * low_half + coeffs[at + s.kz : at + 2 * s.kz] * high_half)
        values = jnp.concatenate(pieces, axis=0)
        return values + pltpu.roll(values, 64, 1), summed

    def mix_forward(values):
        high, low = split(values)
        low_lanes = lane < 64
        packed = jnp.where(low_lanes, high.astype(f32), low.astype(f32)).astype(jnp.bfloat16)
        mixed = jnp.zeros_like(values)
        for t in range(32):
            mixed = mixed + dot(packed, expand[t]) * w2[:, t * 128 : (t + 1) * 128]
        return mixed + pltpu.roll(mixed, 64, 1)

    def mix_adjoint(values):
        mixed = jnp.zeros((2 * s.modes, 128), f32)
        for t in range(32):
            high, low = split(values * w2[:, t * 128 : (t + 1) * 128])
            packed = jnp.concatenate([high, low], axis=0)
            mixed = mixed + lax.dot_general(packed, expand[t], NT, preferred_element_type=f32)
        return mixed[: s.modes] + mixed[s.modes :]

    def scalar_z(i, coeffs):
        pieces = []
        for j in range(2):
            for z in range(2):
                mask = ((lax.div(lane, 2 * s.rows) == 2 * core + j) & (lax.rem(lax.div(lane, s.rows), 2) == z)).astype(f32)
                pieces.append(coeffs[j * s.kz : (j + 1) * s.kz] * mask)
        sent = dot(tzt3[...], tall3(jnp.concatenate(pieces, axis=0)))
        send_pz[i] = sent.reshape(s.gz, 2, 128)
        exchange_gz(lambda p: send_pz.at[i, p], recv_pz.at[i, me_z], spz.at[i], rpz.at[i])

    def scalar_y(i):
        wait(recv_pz.at[i], rpz.at[i])
        arrived = recv_pz[i].reshape(2 * s.gz, 128)
        for d in range(s.gy):
            send_py[i, d] = jnp.broadcast_to(jnp.sum(arrived * ym[d], axis=0, keepdims=True), (8, 128))
        exchange_gy(lambda p: send_py.at[i, p], recv_py.at[i, me_y], spy.at[i], rpy.at[i])

    def scalar_x(i):
        wait(recv_py.at[i], rpy.at[i])
        rows = jnp.concatenate([recv_py[i, h, 0:1, :] for h in range(s.gy)], axis=0)
        columns = rows.T
        field = jnp.zeros((2 * s.rows, 128), f32)
        for a in range(s.kxhi):
            field = field + jnp.dot(
                columns[a * 2 * s.rows : (a + 1) * 2 * s.rows], txk[a], precision=HIGHEST, preferred_element_type=f32
            )
        return field

    def mat(m, field3):
        return dot(field3, mats3[m])

    def over_rows(body, carry):
        return lax.fori_loop(0, s.rows, body, carry, unroll=UNROLL)

    lift_row, bias_one, bias_two, read_row = vec[0:1, :], vec[1:2, :], vec[2:3, :], vec[3:4, :]
    empty = jnp.zeros((1, 128), f32)

    values = modes_kappa * gain_mix
    cells_z(B0K, jnp.concatenate([values[0:8] + bias_mix, values[8:]], axis=0))
    cells_z(B0R, modes_rhs * gain_mix)
    cells_y(B0K)
    cells_y(B0R)
    wait_gy(B0K)

    def first_point(y, carry):
        pre = cells_x(B0K, y) + lift_row * kb[y] + bias_one
        value, slope = gelu_parts(pre)
        act[y] = value
        slope_one[y] = slope
        modes_x(C0A, y, value)
        return carry

    over_rows(first_point, 0)
    unit_gy(C0A)
    wait_gy(B0R)

    def first_tangent(y, carry):
        value = slope_one[y] * (cells_x(B0R, y) + lift_row * rb[y])
        tan[y] = value
        modes_x(C0T, y, value)
        return carry

    over_rows(first_tangent, 0)
    unit_gy(C0T)
    modes_y(C0A)
    modes_y(C0T)
    values, _ = modes_z(C0A)
    cells_z(D0A, mix_forward(values))
    values, _ = modes_z(C0T)
    cells_z(D0T, mix_forward(values))
    cells_y(D0A)
    cells_y(D0T)
    wait_gy(D0A)

    def second_point(y, carry):
        pre = cells_x(D0A, y) + mat(mix_two, flat3(act[y])) + bias_two
        _, slope = gelu_parts(pre)
        slope_two[y] = slope
        return carry

    over_rows(second_point, 0)
    wait_gy(D0T)

    def second_tangent(y, carry):
        slope = slope_two[y]
        tangent = slope * (cells_x(D0T, y) + mat(mix_two, flat3(tan[y])))
        predicted = mat(read_mat, flat3(tangent))
        pred0[y] = predicted
        weighted = wb[y] * predicted
        value = slope * (read_row * weighted)
        back[y] = value
        modes_x(E0, y, value)
        return carry + jnp.sum(weighted * predicted, axis=0, keepdims=True)

    norms = over_rows(second_tangent, empty)
    modes_sum(E0, norms)
    unit_gy(E0)
    modes_y(E0)
    values, curvature = modes_z(E0)
    curvature = curvature * (1.0 / 64.0) + DAMPING * norm_zero
    step_zero = norm_zero / curvature
    cells_z(F0, mix_adjoint(values))
    cells_y(F0)
    wait_gy(F0)

    def local_rows(y, field3):
        rows = lax.dot_general(mats3[4, 0:16, :], field3[:, 0:128], NT, preferred_element_type=f32)
        rows = rows + lax.dot_general(mats3[4, 128:144, :], field3[:, 0:128], NT, preferred_element_type=f32)
        rows = rows + lax.dot_general(mats3[4, 0:16, :], field3[:, 256:384], NT, preferred_element_type=f32)
        return rows

    def first_back(y, carry):
        value = slope_one[y] * (cells_x(F0, y) + mat(mix_back, flat3(back[y])))
        modes_x(G0, y, value)
        value3 = flat3(value)
        rows = local_rows(y, value3)
        lb[0, pl.ds(y, 1), :] = rows[0:1]
        lb[0, pl.ds(s.rows + y, 1), :] = rows[1:2]
        qb[y] = rb[y] * (1.0 - DAMPING * step_zero) - step_zero * mat(lift_mat, value3)
        return carry

    over_rows(first_back, 0)
    unit_gy(G0)
    modes_y(G0)
    values, _ = modes_z(G0)

    coeffs_zero = jnp.sum(values * gain_mix * low_half, axis=1, keepdims=True)
    image = coeffs_zero + jnp.sum(values * lift_row * low_half, axis=1, keepdims=True) + DAMPING * modes_rhs
    modes_res = modes_rhs - step_zero * image
    cells_z(B1, modes_res * gain_mix - (step_zero * coeffs_zero) * lift_row)
    scalar_z(0, coeffs_zero)
    cells_y(B1)
    scalar_y(0)
    wait_gy(B1)

    def next_tangent(y, carry):
        value = slope_one[y] * (cells_x(B1, y) + lift_row * qb[y])
        tan[y] = value
        modes_x(C1, y, value)
        return carry

    over_rows(next_tangent, 0)
    right = rhs[...]
    applied_zero = scalar_x(0) + lb[0] + DAMPING * right
    residual = right - step_zero * applied_zero
    modes_sum(C1, jnp.sum(residual * residual, axis=0, keepdims=True))
    unit_gy(C1)
    modes_y(C1)
    values, norm_one = modes_z(C1)
    cells_z(D1, mix_forward(values))
    ratio = norm_one / norm_zero
    direction = residual + ratio * right
    cells_y(D1)
    wait_gy(D1)

    def next_second(y, carry):
        slope = slope_two[y]
        tangent = slope * (cells_x(D1, y) + mat(mix_two, flat3(tan[y])))
        predicted = mat(read_mat, flat3(tangent))
        value = slope * (read_row * (wb[y] * predicted))
        back[y] = value
        modes_x(E1, y, value)
        moved = predicted + ratio * pred0[y]
        return carry + jnp.sum(wb[y] * moved * moved, axis=0, keepdims=True)

    norms = over_rows(next_second, empty)
    norms = norms * (1.0 / 64.0) + DAMPING * jnp.sum(direction * direction, axis=0, keepdims=True)
    modes_sum(E1, norms)
    unit_gy(E1)
    modes_y(E1)
    values, curvature = modes_z(E1)
    step_one = norm_one / curvature
    cells_z(F1, mix_adjoint(values))
    cells_y(F1)
    wait_gy(F1)

    def next_back(y, carry):
        value = slope_one[y] * (cells_x(F1, y) + mat(mix_back, flat3(back[y])))
        modes_x(G1, y, value)
        rows = local_rows(y, flat3(value))
        lb[1, pl.ds(y, 1), :] = rows[0:1]
        lb[1, pl.ds(s.rows + y, 1), :] = rows[1:2]
        return carry

    over_rows(next_back, 0)
    unit_gy(G1)
    modes_y(G1)
    values, _ = modes_z(G1)
    scalar_z(1, jnp.sum(values * gain_mix * low_half, axis=1, keepdims=True))
    scalar_y(1)
    applied = scalar_x(1) + lb[1] + DAMPING * residual + ratio * applied_zero
    out_solution[...] = step_zero * right + step_one * direction
    out_residual[...] = residual - step_one * applied

    def sent_gy(ref, sem):
        wait(ref, sem)

    for e in range(UNITS):
        wait(send_y.at[e, pl.ds(0, (s.gy - 1) * chunk)], sy.at[e])
        if e in SUMS:
            wait(send_zs.at[SUMS[e], pl.ds(0, s.gz - 1)], sz.at[e])
        else:
            wait(send_z.at[e, pl.ds(0, s.gz - 1)], sz.at[e])
    for i in range(3):
        wait(recv_s.at[i, pl.ds(0, s.gy - 1)], ss.at[i])
    wait(send_a.at[pl.ds(0, s.gy - 1)], sa.at[0])
    wait(recv_az.at[pl.ds(0, s.gz - 1)], sa.at[1])
    for i in range(2):
        wait(send_pz.at[i, pl.ds(0, s.gz - 1)], spz.at[i])
        wait(send_py.at[i, pl.ds(0, s.gy - 1)], spy.at[i])


def local(
    s,
    log_kappa,
    misfit_weight,
    right_side,
    lift_gain,
    lift_bias,
    spec_one,
    spec_two,
    local_one,
    local_two,
    bias_one,
    bias_two,
    readout,
):
    shape = log_kappa.shape
    rows = lambda x: x.reshape(2 * s.rows, s.line)
    lift_local = jnp.dot(lift_gain, local_one, precision=HIGHEST)
    bias_local = jnp.dot(lift_bias, local_one, precision=HIGHEST)
    vec = jnp.stack([lift_local, bias_local + bias_one, bias_two, readout])
    vec = jnp.concatenate([vec, vec], axis=1)
    vec = jnp.concatenate([vec, jnp.zeros_like(vec)], axis=0)
    gexp = jnp.repeat(jnp.stack([lift_gain, lift_bias]), 64, axis=1)
    gexp = jnp.concatenate([gexp, jnp.zeros((6, 4096), jnp.float32)], axis=0)
    same = np.kron(np.eye(2, dtype=np.float32), np.ones((64, 64), np.float32))
    column = lambda v: jnp.broadcast_to(jnp.concatenate([v, v])[:, None], (128, 128))
    two_rows = jnp.concatenate([same[0:1], same[64:65], jnp.zeros((126, 128), jnp.float32)], axis=0) * vec[0:1]
    mats = jnp.stack(
        [
            jnp.tile(local_two, (2, 2)) * same,
            jnp.tile(local_two.T, (2, 2)) * same,
            column(readout) * same,
            column(lift_local) * same,
            two_rows,
        ]
    )
    operands = [
        rows(log_kappa), rows(misfit_weight), rows(right_side), vec, gexp,
        spec_one.reshape(s.modes, 4096), spec_two.reshape(s.modes, 4096), mats,
    ] + [jnp.asarray(t) for t in tables_of(s)]
    f32, bf16 = jnp.float32, jnp.bfloat16
    vmem = lambda *dims: pltpu.VMEM(dims, f32)
    half = s.kx * s.rows
    cell = (s.rows, 128, 128)
    scratch = [
        vmem(UNITS, half, 128), vmem(UNITS, half, 128),
        vmem(UNITS, s.gz, 2, 128), vmem(UNITS, s.gz, 2, 128),
        vmem(3, s.gz, 4, 128), vmem(3, s.gz, 4, 128),
        vmem(3, 8, 128), vmem(3, s.gy, 8, 128),
        vmem(s.gy, 8, 128), vmem(s.gy, 8, 128),
        vmem(2, 4, 128), vmem(s.gz, 4, 128),
        vmem(2, s.gz, 2, 128), vmem(2, s.gz, 2, 128),
        vmem(2, s.gy, 8, 128), vmem(2, s.gy, 8, 128),
        pltpu.VMEM((5, 384, 128), bf16),
    ] + [vmem(*cell) for _ in range(10)] + [vmem(2, 2 * s.rows, 128)]
    counts = [UNITS] * 4 + [3, 3, 2, 2, 2, 2, 2, 2]
    scratch += [pltpu.SemaphoreType.DMA((n,)) for n in counts]
    results = pl.pallas_call(
        functools.partial(kernel, s),
        out_shape=[jax.ShapeDtypeStruct((2 * s.rows, s.line), f32)] * 2,
        in_specs=[pl.BlockSpec(memory_space=pltpu.VMEM)] * len(operands),
        out_specs=[pl.BlockSpec(memory_space=pltpu.VMEM)] * 2,
        scratch_shapes=scratch,
        compiler_params=pltpu.CompilerParams(
            collective_id=0, has_side_effects=True, vmem_limit_bytes=60 * 1024 * 1024
        ),
        name="two_steps",
    )(*operands)
    return tuple(x.reshape(shape) for x in results)


def solution(mesh, kx=KX, ky=KY, kz=KZ, rows=16, line=128):
    s = Sizes(mesh.shape["gz"], mesh.shape["gy"], rows, line, kx, ky, kz)
    field = P("gz", "gy", None)
    weights = P("gz", "gy", None, None)
    return jax.shard_map(
        functools.partial(local, s),
        mesh=mesh,
        in_specs=(field, field, field, P(), P(), weights, weights, P(), P(), P(), P(), P()),
        out_specs=(field, field),
        check_vma=False,
    )
```

```python
import functools
import math

import jax
import jax.numpy as jnp
import ml_dtypes
import numpy as np
from jax import lax
from jax.experimental import pallas as pl
from jax.experimental.pallas import tpu as pltpu
from jax.sharding import PartitionSpec as P

KX = 32
KY = 32
KZ = 32
DAMPING = 0.3
HIGHEST = lax.Precision.HIGHEST
MESH = pl.DeviceIdType.MESH
NT = (((1,), (1,)), ((), ()))
UNITS = 15
B0K, B0R, C0A, C0T, D0A, D0T, E0, F0, G0, B1, C1, D1, E1, F1, G1 = range(UNITS)
SUMS = {E0: 0, C1: 1, E1: 2}
PIECES = 4


def basis_table(modes, length):
    mode_index = np.arange(modes)
    frequency = (mode_index + 1) // 2
    phase_steps = frequency[:, None] * np.arange(length)[None, :] % length
    angles = phase_steps * (2.0 * math.pi / length)
    is_sine = (mode_index % 2 == 0) & (mode_index > 0)
    scales = np.where(mode_index == 0, math.sqrt(1.0 / length), math.sqrt(2.0 / length))
    return (np.where(is_sine[:, None], np.sin(angles), np.cos(angles)) * scales[:, None]).astype(np.float32)


def parts_of(table):
    high = table.astype(ml_dtypes.bfloat16)
    low = (table - high.astype(np.float32)).astype(ml_dtypes.bfloat16)
    return high, low


def wide(table):
    high, low = parts_of(table)
    return np.concatenate([high, low, high], axis=1)


class Sizes:
    def __init__(self, gz, gy, rows, line, kx, ky, kz):
        self.gz, self.gy, self.rows, self.line = gz, gy, rows, line
        self.kx, self.ky, self.kz = kx, ky, kz
        self.kxhi = kx // gy
        self.modes = ky * self.kxhi // gz * kz
        self.nx = 4 if gz >= 32 else 1
        self.ny = gz // 2 // self.nx
        self.deep = rows // PIECES
        self.block = kx * self.deep
        self.part = self.kxhi * self.deep


def tables_of(s):
    bx, by, bz = basis_table(s.kx, s.line), basis_table(s.ky, s.rows * s.gy), basis_table(s.kz, 2 * s.gz)
    order = np.arange(s.kx).reshape(s.kxhi, s.gy).T.reshape(-1)
    tx = bx[order]
    eye = np.eye(s.kxhi, dtype=np.float32)
    byd = by.reshape(s.ky, s.gy, s.rows)
    byp = by.reshape(s.ky, s.gy, PIECES, s.deep)
    ty = np.einsum("kdpy,ab->pkadby", byp, eye).reshape(PIECES, s.ky * s.kxhi, s.block)
    tyt = np.einsum("kdpy,ab->pdbyka", byp, eye).reshape(PIECES * s.block, s.ky * s.kxhi)
    bzg = bz.reshape(s.kz, s.gz, 2)
    two = np.eye(2, dtype=np.float32)
    tz = np.einsum("kgz,ij->izkgj", bzg, two).reshape(4 * s.kz, 2 * s.gz)
    tza = np.einsum("kgz,ij->izkgj", bzg, np.eye(2, 4, dtype=np.float32)).reshape(4 * s.kz, 4 * s.gz)
    ma = np.zeros((s.gy, 2, 2, s.rows, s.ky, 2, 2), np.float32)
    for f in range(2):
        for z in range(2):
            ma[:, f, z, :, :, z, f] = byd.transpose(1, 2, 0)
    ma = ma.reshape(s.gy, 4 * s.rows, 4 * s.ky)
    full = np.zeros((s.gy, 128, 128), np.float32)
    full[:, : 4 * s.rows, : 4 * s.ky] = ma
    ym = np.broadcast_to(byd.transpose(1, 0, 2)[:, :, None, None, None, :], (s.gy, s.ky, s.kxhi, s.kxhi, 2, s.rows))
    ym = np.ascontiguousarray(ym).reshape(s.gy, s.ky * s.kxhi, s.kxhi * 2 * s.rows)
    lanes = np.arange(128)
    expand = (np.arange(128)[None, :, None] % 64 == 2 * np.arange(32)[:, None, None] + lanes[None, None, :] // 64)
    return [
        tx,
        bx.reshape(s.kxhi, s.gy, s.line),
        wide(tx),
        wide(np.ascontiguousarray(tx.T)),
        np.stack([wide(t) for t in ty]),
        wide(tyt),
        wide(tz),
        wide(np.ascontiguousarray(tz.T)),
        tza,
        full,
        ym,
        expand.astype(ml_dtypes.bfloat16),
        np.concatenate([np.eye(64, dtype=np.float32)] * 2, axis=1),
    ]


def split(x):
    high = x.astype(jnp.bfloat16)
    return high, (x - high.astype(jnp.float32)).astype(jnp.bfloat16)


def tall3(x):
    high, low = split(x)
    return jnp.concatenate([high, high, low], axis=0)


def flat3(x):
    high, low = split(x)
    return jnp.concatenate([high, high, low], axis=1)


def dot(a, b):
    return jnp.dot(a, b, preferred_element_type=jnp.float32)


def gelu_parts(grid_field):
    normal_cdf = 0.5 * (1.0 + lax.erf(grid_field * (1.0 / math.sqrt(2.0))))
    density = jnp.exp(-0.5 * grid_field * grid_field) * (1.0 / math.sqrt(2.0 * math.pi))
    return (grid_field * normal_cdf, normal_cdf + grid_field * density)


def total(x):
    return jnp.sum(jnp.sum(x, axis=0, keepdims=True), axis=1, keepdims=True)


def kernel(s, *refs):
    (kappa, weight, rhs, gain_in, bias_in, b1_in, b2_in, read_in, l1_in, l2_in, tx, txk, tx3, txt3, tz3, tzt3, twice,
     w1_in, w2_in, ty3_in, tyt3_in, tza_in, ma_in, ym_in, expand_in,
     out_solution, out_residual,
     send_y, recv_y, send_z, recv_z, send_zs, recv_zs, send_s, recv_s,
     send_a, recv_a, send_az, recv_az, send_pz, recv_pz, send_py, recv_py,
     mats3, kb, rb, wb, slope_one, slope_two, act, tan, back, pred0, qb, lb, vecs,
     w1, w2, ty3, tyt3, tza, ma, ym, expand,
     sy, ry, sz, rz, ss, rs, sa, ra, spz, rpz, spy, rpy, loads) = refs
    me_z, me_y = lax.axis_index("gz"), lax.axis_index("gy")
    core, chip = lax.rem(me_z, 2), lax.div(me_z, 2)
    at_y, at_x = lax.div(chip, s.nx), lax.rem(chip, s.nx)
    f32 = jnp.float32

    brought = {}
    for i, (src, dst) in enumerate(
        ((ma_in, ma), (expand_in, expand), (w1_in, w1), (tza_in, tza), (tyt3_in, tyt3), (ty3_in, ty3), (w2_in, w2), (ym_in, ym))
    ):
        brought[id(dst)] = pltpu.make_async_copy(src, dst, loads.at[i])
        brought[id(dst)].start()

    def ready(dst):
        brought[id(dst)].wait()

    ring_x = sorted(range(s.nx), key=lambda k: -min(k, s.nx - k))

    def peers_gz(visit):
        def at(dy, dx, dc):
            y, x = lax.rem(at_y + dy, s.ny), lax.rem(at_x + dx, s.nx)
            visit((y * s.nx + x) * 2 + lax.rem(core + dc, 2))

        def step(i, carry):
            dy = s.ny // 2 + lax.div(i + 1, 2) * (1 - 2 * lax.rem(i, 2))
            for dx in ring_x:
                for dc in range(2):
                    at(dy, dx, dc)
            return carry

        lax.fori_loop(0, s.ny - 1, step, 0)
        for dx in ring_x:
            for dc in range(2):
                if dx or dc:
                    at(0, dx, dc)

    hops = sorted(range(1, s.gy), key=lambda k: -min(k, s.gy - k))
    barrier = pltpu.get_barrier_semaphore()
    for k in hops:
        pl.semaphore_signal(barrier, inc=1, device_id={"gy": lax.rem(me_y + k, s.gy)}, device_id_type=MESH)

    peers_gz(lambda p: pl.semaphore_signal(barrier, inc=1, device_id={"gz": p}, device_id_type=MESH))

    def exchange_gy(src_of, dst, send_sem, recv_sem):
        for k in hops:
            peer = lax.rem(me_y + k, s.gy)
            pltpu.make_async_remote_copy(
                src_of(peer), dst, send_sem, recv_sem, device_id={"gy": peer}, device_id_type=MESH
            ).start()
        pltpu.make_async_copy(src_of(me_y), dst, recv_sem).start()

    def exchange_gz(src_of, dst, send_sem, recv_sem):
        peers_gz(
            lambda p: pltpu.make_async_remote_copy(
                src_of(p), dst, send_sem, recv_sem, device_id={"gz": p}, device_id_type=MESH
            ).start()
        )
        pltpu.make_async_copy(src_of(me_z), dst, recv_sem).start()

    def wait(ref, sem):
        pltpu.make_async_copy(ref, ref, sem).wait()

    def piece(p):
        return slice(p * s.block, (p + 1) * s.block)

    def piece_gy(e, p):
        exchange_gy(
            lambda d: send_y.at[e, pl.ds(pl.multiple_of(p * s.block + d * s.part, s.part), s.part)],
            recv_y.at[e, pl.ds(pl.multiple_of(p * s.block + me_y * s.part, s.part), s.part)],
            sy.at[e], ry.at[e, p],
        )

    def wait_gy(e, p):
        wait(recv_y.at[e, pl.ds(p * s.block, s.block)], ry.at[e, p])

    def unit_gz(e):
        if e in SUMS:
            i = SUMS[e]
            exchange_gz(lambda p: send_zs.at[i, p], recv_zs.at[i, me_z], sz.at[e], rz.at[e])
        else:
            exchange_gz(lambda p: send_z.at[e, p], recv_z.at[e, me_z], sz.at[e], rz.at[e])

    def wait_gz(e):
        if e in SUMS:
            wait(recv_zs.at[SUMS[e]], rz.at[e])
        else:
            wait(recv_z.at[e], rz.at[e])

    lane = lax.broadcasted_iota(jnp.int32, (1, 128), 1)
    low_half = (lane < 64).astype(f32)
    high_half = 1.0 - low_half

    both = jnp.concatenate([kappa[...], rhs[...], jnp.zeros((128 - 4 * s.rows, 128), f32)], axis=0)
    spectrum = lax.dot_general(tx[...], both, NT, precision=HIGHEST, preferred_element_type=f32)
    own = jnp.sum(rhs[...] * rhs[...], axis=0, keepdims=True)
    send_a[...] = jnp.zeros_like(send_a)
    for h in range(s.gy):
        send_a[h, 0 : s.kxhi, :] = spectrum[h * s.kxhi : (h + 1) * s.kxhi]
        send_a[h, s.kxhi : s.kxhi + 1, :] = own
    vecs[...] = jnp.zeros_like(vecs)
    for i, ref in enumerate((gain_in, bias_in, b1_in, b2_in, read_in)):
        vecs[i : i + 1, :] = ref[...]
    exact = functools.partial(jnp.dot, precision=HIGHEST, preferred_element_type=f32)
    doubled = exact(vecs[...], twice[...])
    lifted = exact(exact(vecs[...], l1_in[...]), twice[...])
    gain_row, read_row, bias_two = doubled[0:1], doubled[4:5], doubled[3:4]
    lift_row, bias_one = lifted[0:1], lifted[1:2] + doubled[2:3]
    same = lax.div(lax.broadcasted_iota(jnp.int32, (128, 128), 0), 64) == lax.div(
        lax.broadcasted_iota(jnp.int32, (128, 128), 1), 64
    )
    only = lambda x: jnp.where(same, x, 0.0)
    column = lambda x: only(jnp.broadcast_to(x, (128, 128)).T)
    local_two = only(jnp.concatenate([exact(l2_in[...], twice[...])] * 2, axis=0))
    row = lax.broadcasted_iota(jnp.int32, (128, 128), 0)
    two_rows = jnp.where((row == 0) & (lane < 64) | (row == 1) & (lane >= 64), jnp.broadcast_to(lift_row, (128, 128)), 0.0)
    pl.semaphore_wait(barrier, s.gy + s.gz - 2)
    exchange_gy(lambda p: send_a.at[p], recv_a.at[me_y], sa.at[0], ra.at[0])

    for m, table in enumerate((local_two, local_two.T, column(read_row), column(lift_row), two_rows)):
        high, low = split(table)
        mats3[m, 0:128, :] = high
        mats3[m, 128:256, :] = low
        mats3[m, 256:384, :] = high
    mix_two, mix_back, read_mat, lift_mat = range(4)

    gain_mix = jnp.zeros((s.modes, 128), f32)
    bias_mix = jnp.zeros((8, 128), f32)
    high, low = split(doubled)
    packed = jnp.where(lane < 64, high.astype(f32), low.astype(f32)).astype(jnp.bfloat16)
    ready(expand)
    ready(w1)
    for t in range(32):
        spread_rows = dot(packed, expand[t])
        gain_mix = gain_mix + w1[:, t * 128 : (t + 1) * 128] * spread_rows[0:1]
        bias_mix = bias_mix + w1[0:8, t * 128 : (t + 1) * 128] * spread_rows[1:2]
    gain_mix = gain_mix + pltpu.roll(gain_mix, 64, 1)
    bias_mix = bias_mix + pltpu.roll(bias_mix, 64, 1)
    is_mean = ((me_z == 0) & (me_y == 0)).astype(f32)
    first_row = (lax.broadcasted_iota(jnp.int32, (8, 128), 0) == 0).astype(f32)
    volume = math.sqrt(float(2 * s.gz) * float(s.rows * s.gy) * float(s.line))
    bias_mix = bias_mix * first_row * (is_mean * volume)

    ready(ma)
    wait(recv_a, ra.at[0])
    mixed = jnp.zeros((8, 128), f32)
    own = jnp.zeros((1, 128), f32)
    for d in range(s.gy):
        mixed = mixed + jnp.dot(recv_a[d], ma[d], precision=HIGHEST, preferred_element_type=f32)
        own = own + recv_a[d, s.kxhi : s.kxhi + 1, :]
    for c in range(2):
        send_az[c, 0:2, :] = mixed[2 * c : 2 * c + 2]
        send_az[c, 2:3, :] = own
        send_az[c, 3:4, :] = jnp.zeros((1, 128), f32)
    exchange_gz(lambda p: send_az.at[lax.rem(p, 2)], recv_az.at[me_z], sa.at[1], ra.at[1])

    def spread(p, carry):
        for src, dst in ((kappa, kb), (rhs, rb), (weight, wb)):
            for y in range(s.deep):
                near = jnp.broadcast_to(src[pl.ds(p * s.deep + y, 1), :], (64, 128))
                far = jnp.broadcast_to(src[pl.ds(s.rows + p * s.deep + y, 1), :], (64, 128))
                dst[p, :, y * 128 : (y + 1) * 128] = jnp.concatenate([near, far], axis=0).T
        return carry

    lax.fori_loop(0, PIECES, spread, 0)

    ready(tza)
    wait(recv_az, ra.at[1])
    arrived = recv_az[...].reshape(4 * s.gz, 128)
    row = lax.broadcasted_iota(jnp.int32, (4 * s.gz, 128), 0)
    norm_zero = total(jnp.where(lax.rem(row, 4) == 2, arrived, 0.0))
    coeffs = jnp.dot(tza[...], arrived, precision=HIGHEST, preferred_element_type=f32)

    def pick(f):
        columns = []
        for j in range(2):
            kept = jnp.zeros((s.kz, 128), f32)
            for z in range(2):
                at = (2 * j + z) * s.kz
                kept = kept + coeffs[at : at + s.kz] * (lane == chip * 4 + z * 2 + f).astype(f32)
            columns.append(jnp.sum(kept, axis=1, keepdims=True))
        return jnp.concatenate(columns, axis=0)

    modes_kappa, modes_rhs = pick(0), pick(1)

    def cells_z(e, values):
        pieces = []
        for j in range(2):
            half = values[j * s.kz : (j + 1) * s.kz]
            pieces += [half * low_half, half * high_half]
        sent = dot(tzt3[...], tall3(jnp.concatenate(pieces, axis=0)))
        send_z[e] = sent.reshape(s.gz, 2, 128)
        unit_gz(e)

    def cells_y(e):
        wait_gz(e)
        values = tall3(recv_z[e].reshape(2 * s.gz, 128))
        for p in range(PIECES):
            send_y[e, piece(p), :] = dot(tyt3[piece(p), :], values)
            piece_gy(e, p)

    def cells_x(e, p):
        wait_gy(e, p)
        rows = [recv_y[e, pl.ds(p * s.block + y, s.kx, stride=s.deep), :] for y in range(s.deep)]
        return dot(txt3[...], tall3(jnp.concatenate(rows, axis=1)))

    def modes_x(e, p, parts):
        high, low = parts
        sent = dot(tx3[...], jnp.concatenate([high, high, low], axis=0))
        for y in range(s.deep):
            send_y[e, pl.ds(p * s.block + y, s.kx, stride=s.deep), :] = sent[:, y * 128 : (y + 1) * 128]
        piece_gy(e, p)

    def modes_sum(e, partial):
        i = SUMS[e]
        send_s[i] = jnp.broadcast_to(partial, (8, 128))
        exchange_gy(lambda p: send_s.at[i], recv_s.at[i, me_y], ss.at[i], rs.at[i])

    def modes_y(e):
        sent = jnp.zeros((2 * s.gz, 128), f32)
        for p in range(PIECES):
            wait_gy(e, p)
            sent = sent + dot(ty3[p], tall3(recv_y[e, piece(p), :]))
        sent = sent.reshape(s.gz, 2, 128)
        if e in SUMS:
            i = SUMS[e]
            wait(recv_s.at[i], rs.at[i])
            partial = jnp.zeros((1, 128), f32)
            for d in range(s.gy):
                partial = partial + recv_s[i, d, 0:1, :]
            send_zs[i, :, 0:2, :] = sent
            send_zs[i, :, 2:4, :] = jnp.broadcast_to(partial[None], (s.gz, 2, 128))
        else:
            send_z[e] = sent
        unit_gz(e)

    def modes_z(e):
        wait_gz(e)
        summed = None
        if e in SUMS:
            i = SUMS[e]
            arrived = recv_zs[i, :, 0:2, :].reshape(2 * s.gz, 128)
            summed = total(recv_zs[i, :, 2:3, :].reshape(s.gz, 128))
        else:
            arrived = recv_z[e].reshape(2 * s.gz, 128)
        coeffs = dot(tz3[...], tall3(arrived))
        pieces = []
        for j in range(2):
            at = 2 * j * s.kz
            pieces.append(coeffs[at : at + s.kz] * low_half + coeffs[at + s.kz : at + 2 * s.kz] * high_half)
        values = jnp.concatenate(pieces, axis=0)
        return values + pltpu.roll(values, 64, 1), summed

    def mix_forward(values):
        high, low = split(values)
        low_lanes = lane < 64
        packed = jnp.where(low_lanes, high.astype(f32), low.astype(f32)).astype(jnp.bfloat16)
        mixed = jnp.zeros_like(values)
        for t in range(32):
            mixed = mixed + dot(packed, expand[t]) * w2[:, t * 128 : (t + 1) * 128]
        return mixed + pltpu.roll(mixed, 64, 1)

    def mix_adjoint(values):
        mixed = jnp.zeros((2 * s.modes, 128), f32)
        for t in range(32):
            high, low = split(values * w2[:, t * 128 : (t + 1) * 128])
            packed = jnp.concatenate([high, low], axis=0)
            mixed = mixed + lax.dot_general(packed, expand[t], NT, preferred_element_type=f32)
        return mixed[: s.modes] + mixed[s.modes :]

    def scalar_z(i, coeffs):
        pieces = []
        for j in range(2):
            for z in range(2):
                mask = ((lax.div(lane, 2 * s.rows) == 2 * core + j) & (lax.rem(lax.div(lane, s.rows), 2) == z)).astype(f32)
                pieces.append(coeffs[j * s.kz : (j + 1) * s.kz] * mask)
        sent = dot(tzt3[...], tall3(jnp.concatenate(pieces, axis=0)))
        send_pz[i] = sent.reshape(s.gz, 2, 128)
        exchange_gz(lambda p: send_pz.at[i, p], recv_pz.at[i, me_z], spz.at[i], rpz.at[i])

    def scalar_y(i):
        wait(recv_pz.at[i], rpz.at[i])
        arrived = recv_pz[i].reshape(2 * s.gz, 128)
        for d in range(s.gy):
            send_py[i, d] = jnp.broadcast_to(jnp.sum(arrived * ym[d], axis=0, keepdims=True), (8, 128))
        exchange_gy(lambda p: send_py.at[i, p], recv_py.at[i, me_y], spy.at[i], rpy.at[i])

    def scalar_x(i):
        wait(recv_py.at[i], rpy.at[i])
        rows = jnp.concatenate([recv_py[i, h, 0:1, :] for h in range(s.gy)], axis=0)
        columns = rows.T
        field = jnp.zeros((2 * s.rows, 128), f32)
        for a in range(s.kxhi):
            field = field + jnp.dot(
                columns[a * 2 * s.rows : (a + 1) * 2 * s.rows], txk[a], precision=HIGHEST, preferred_element_type=f32
            )
        return field

    def lines(x):
        return jnp.concatenate([x[:, y * 128 : (y + 1) * 128] for y in range(s.deep)], axis=0)

    def across(x):
        return jnp.concatenate([x[y * 128 : (y + 1) * 128] for y in range(s.deep)], axis=1)

    def mat(m, parts):
        high, low = lines(parts[0]), lines(parts[1])
        return across(dot(jnp.concatenate([high, high, low], axis=1), mats3[m]))

    def fold(x):
        x = jnp.sum(x, axis=0, keepdims=True)
        return sum(x[:, y * 128 : (y + 1) * 128] for y in range(s.deep))

    def local_rows(i, p, parts):
        high, low = lines(parts[0]), lines(parts[1])
        rows = lax.dot_general(mats3[4, 0:16, :], high, NT, preferred_element_type=f32)
        rows = rows + lax.dot_general(mats3[4, 128:144, :], high, NT, preferred_element_type=f32)
        rows = rows + lax.dot_general(mats3[4, 0:16, :], low, NT, preferred_element_type=f32)
        for y in range(s.deep):
            lb[i, p * s.deep + y : p * s.deep + y + 1, :] = rows[0:1, y * 128 : (y + 1) * 128]
            at = s.rows + p * s.deep + y
            lb[i, at : at + 1, :] = rows[1:2, y * 128 : (y + 1) * 128]

    wide_row = lambda x: jnp.concatenate([x] * s.deep, axis=1)
    lift_wide, one_wide, two_wide, read_wide = map(wide_row, (lift_row, bias_one, bias_two, read_row))
    empty = jnp.zeros((1, 128), f32)

    values = modes_kappa * gain_mix
    cells_z(B0K, jnp.concatenate([values[0:8] + bias_mix, values[8:]], axis=0))
    cells_z(B0R, modes_rhs * gain_mix)
    ready(tyt3)
    cells_y(B0K)
    cells_y(B0R)
    for p in range(PIECES):
        value, slope = gelu_parts(cells_x(B0K, p) + lift_wide * kb[p] + one_wide)
        act[p] = value
        slope_one[p] = slope
        modes_x(C0A, p, split(value))
    for p in range(PIECES):
        value = slope_one[p] * (cells_x(B0R, p) + lift_wide * rb[p])
        tan[p] = value
        modes_x(C0T, p, split(value))
    ready(ty3)
    modes_y(C0A)
    modes_y(C0T)
    ready(w2)
    values, _ = modes_z(C0A)
    cells_z(D0A, mix_forward(values))
    values, _ = modes_z(C0T)
    cells_z(D0T, mix_forward(values))
    cells_y(D0A)
    cells_y(D0T)
    for p in range(PIECES):
        _, slope = gelu_parts(cells_x(D0A, p) + mat(mix_two, split(act[p])) + two_wide)
        slope_two[p] = slope
    norms = empty
    for p in range(PIECES):
        slope = slope_two[p]
        tangent = slope * (cells_x(D0T, p) + mat(mix_two, split(tan[p])))
        predicted = mat(read_mat, split(tangent))
        pred0[p] = predicted
        weighted = wb[p] * predicted
        value = slope * (read_wide * weighted)
        back[p] = value
        modes_x(E0, p, split(value))
        norms = norms + fold(weighted * predicted)
    modes_sum(E0, norms)
    modes_y(E0)
    values, curvature = modes_z(E0)
    curvature = curvature * (1.0 / 64.0) + DAMPING * norm_zero
    step_zero = norm_zero / curvature
    cells_z(F0, mix_adjoint(values))
    cells_y(F0)
    for p in range(PIECES):
        value = slope_one[p] * (cells_x(F0, p) + mat(mix_back, split(back[p])))
        parts = split(value)
        modes_x(G0, p, parts)
        local_rows(0, p, parts)
        qb[p] = rb[p] * (1.0 - DAMPING * step_zero) - step_zero * mat(lift_mat, parts)
    modes_y(G0)
    values, _ = modes_z(G0)

    coeffs_zero = jnp.sum(values * gain_mix * low_half, axis=1, keepdims=True)
    image = coeffs_zero + jnp.sum(values * lift_row * low_half, axis=1, keepdims=True) + DAMPING * modes_rhs
    modes_res = modes_rhs - step_zero * image
    cells_z(B1, modes_res * gain_mix - (step_zero * coeffs_zero) * lift_row)
    scalar_z(0, coeffs_zero)
    cells_y(B1)
    ready(ym)
    scalar_y(0)
    for p in range(PIECES):
        value = slope_one[p] * (cells_x(B1, p) + lift_wide * qb[p])
        tan[p] = value
        modes_x(C1, p, split(value))
    right = rhs[...]
    applied_zero = scalar_x(0) + lb[0] + DAMPING * right
    residual = right - step_zero * applied_zero
    modes_sum(C1, jnp.sum(residual * residual, axis=0, keepdims=True))
    modes_y(C1)
    values, norm_one = modes_z(C1)
    cells_z(D1, mix_forward(values))
    ratio = norm_one / norm_zero
    direction = residual + ratio * right
    cells_y(D1)
    norms = empty
    for p in range(PIECES):
        slope = slope_two[p]
        tangent = slope * (cells_x(D1, p) + mat(mix_two, split(tan[p])))
        predicted = mat(read_mat, split(tangent))
        value = slope * (read_wide * (wb[p] * predicted))
        back[p] = value
        modes_x(E1, p, split(value))
        moved = predicted + ratio * pred0[p]
        norms = norms + fold(wb[p] * moved * moved)
    norms = norms * (1.0 / 64.0) + DAMPING * jnp.sum(direction * direction, axis=0, keepdims=True)
    modes_sum(E1, norms)
    modes_y(E1)
    values, curvature = modes_z(E1)
    step_one = norm_one / curvature
    cells_z(F1, mix_adjoint(values))
    cells_y(F1)
    for p in range(PIECES):
        value = slope_one[p] * (cells_x(F1, p) + mat(mix_back, split(back[p])))
        parts = split(value)
        modes_x(G1, p, parts)
        local_rows(1, p, parts)
    modes_y(G1)
    values, _ = modes_z(G1)
    scalar_z(1, jnp.sum(values * gain_mix * low_half, axis=1, keepdims=True))
    scalar_y(1)
    applied = scalar_x(1) + lb[1] + DAMPING * residual + ratio * applied_zero
    out_solution[...] = step_zero * right + step_one * direction
    out_residual[...] = residual - step_one * applied

    for e in range(UNITS):
        wait(send_y.at[e, pl.ds(0, PIECES * (s.gy - 1) * s.part)], sy.at[e])
        if e in SUMS:
            wait(send_zs.at[SUMS[e], pl.ds(0, s.gz - 1)], sz.at[e])
        else:
            wait(send_z.at[e, pl.ds(0, s.gz - 1)], sz.at[e])
    for i in range(3):
        wait(recv_s.at[i, pl.ds(0, s.gy - 1)], ss.at[i])
    wait(send_a.at[pl.ds(0, s.gy - 1)], sa.at[0])
    wait(recv_az.at[pl.ds(0, s.gz - 1)], sa.at[1])
    for i in range(2):
        wait(send_pz.at[i, pl.ds(0, s.gz - 1)], spz.at[i])
        wait(send_py.at[i, pl.ds(0, s.gy - 1)], spy.at[i])


def local(
    s,
    log_kappa,
    misfit_weight,
    right_side,
    lift_gain,
    lift_bias,
    spec_one,
    spec_two,
    local_one,
    local_two,
    bias_one,
    bias_two,
    readout,
):
    shape = log_kappa.shape
    rows = lambda x: x.reshape(2 * s.rows, s.line)
    row = lambda x: x.reshape(1, 64)
    tables = [jnp.asarray(t) for t in tables_of(s)]
    tx, txk, tx3, txt3, ty3, tyt3, tz3, tzt3, tza, ma, ym, expand, twice = tables
    near = [
        rows(log_kappa), rows(misfit_weight), rows(right_side),
        row(lift_gain), row(lift_bias), row(bias_one), row(bias_two), row(readout),
        local_one, local_two, tx, txk, tx3, txt3, tz3, tzt3, twice,
    ]
    far = [spec_one.reshape(s.modes, 4096), spec_two.reshape(s.modes, 4096), ty3, tyt3, tza, ma, ym, expand]
    f32, bf16 = jnp.float32, jnp.bfloat16
    vmem = lambda *dims: pltpu.VMEM(dims, f32)
    half = s.kx * s.rows
    cell = (PIECES, 128, 128 * s.deep)
    scratch = [
        vmem(UNITS, half, 128), vmem(UNITS, half, 128),
        vmem(UNITS, s.gz, 2, 128), vmem(UNITS, s.gz, 2, 128),
        vmem(3, s.gz, 4, 128), vmem(3, s.gz, 4, 128),
        vmem(3, 8, 128), vmem(3, s.gy, 8, 128),
        vmem(s.gy, 8, 128), vmem(s.gy, 8, 128),
        vmem(2, 4, 128), vmem(s.gz, 4, 128),
        vmem(2, s.gz, 2, 128), vmem(2, s.gz, 2, 128),
        vmem(2, s.gy, 8, 128), vmem(2, s.gy, 8, 128),
        pltpu.VMEM((5, 384, 128), bf16),
    ] + [vmem(*cell) for _ in range(10)] + [vmem(2, 2 * s.rows, 128), vmem(8, 64)]
    scratch += [pltpu.VMEM(x.shape, x.dtype) for x in far]
    counts = [(UNITS,), (UNITS, PIECES), (UNITS,), (UNITS,), (3,), (3,), (2,), (2,), (2,), (2,), (2,), (2,), (len(far),)]
    scratch += [pltpu.SemaphoreType.DMA(n) for n in counts]
    results = pl.pallas_call(
        functools.partial(kernel, s),
        out_shape=[jax.ShapeDtypeStruct((2 * s.rows, s.line), f32)] * 2,
        in_specs=[pl.BlockSpec(memory_space=pltpu.VMEM)] * len(near) + [pl.BlockSpec(memory_space=pl.ANY)] * len(far),
        out_specs=[pl.BlockSpec(memory_space=pltpu.VMEM)] * 2,
        scratch_shapes=scratch,
        compiler_params=pltpu.CompilerParams(
            collective_id=0, has_side_effects=True, vmem_limit_bytes=60 * 1024 * 1024
        ),
        name="two_steps",
    )(*near, *far)
    return tuple(x.reshape(shape) for x in results)


def solution(mesh, kx=KX, ky=KY, kz=KZ, rows=16, line=128):
    s = Sizes(mesh.shape["gz"], mesh.shape["gy"], rows, line, kx, ky, kz)
    field = P("gz", "gy", None)
    weights = P("gz", "gy", None, None)
    return jax.shard_map(
        functools.partial(local, s),
        mesh=mesh,
        in_specs=(field, field, field, P(), P(), weights, weights, P(), P(), P(), P(), P()),
        out_specs=(field, field),
        check_vma=False,
    )
```

```python
import functools
import math

import jax
import jax.numpy as jnp
import ml_dtypes
import numpy as np
from jax import lax
from jax.experimental import pallas as pl
from jax.experimental.pallas import tpu as pltpu
from jax.sharding import PartitionSpec as P

KX = 32
KY = 32
KZ = 32
DAMPING = 0.3
HIGHEST = lax.Precision.HIGHEST
MESH = pl.DeviceIdType.MESH
NT = (((1,), (1,)), ((), ()))
UNITS = 15
B0K, B0R, C0A, C0T, D0A, D0T, E0, F0, G0, B1, C1, D1, E1, F1, G1 = range(UNITS)
SUMS = {E0: 0, C1: 1, E1: 2}
PIECES = 4
NX = 4


def basis_table(modes, length):
    mode_index = np.arange(modes)
    frequency = (mode_index + 1) // 2
    phase_steps = frequency[:, None] * np.arange(length)[None, :] % length
    angles = phase_steps * (2.0 * math.pi / length)
    is_sine = (mode_index % 2 == 0) & (mode_index > 0)
    scales = np.where(mode_index == 0, math.sqrt(1.0 / length), math.sqrt(2.0 / length))
    return (np.where(is_sine[:, None], np.sin(angles), np.cos(angles)) * scales[:, None]).astype(np.float32)


def parts_of(table):
    high = table.astype(ml_dtypes.bfloat16)
    low = (table - high.astype(np.float32)).astype(ml_dtypes.bfloat16)
    return high, low


def wide(table):
    high, low = parts_of(table)
    return np.concatenate([high, low, high], axis=1)


class Sizes:
    def __init__(self, gz, gy, rows, line, kx, ky, kz):
        self.gz, self.gy, self.rows, self.line = gz, gy, rows, line
        self.kx, self.ky, self.kz = kx, ky, kz
        self.modes = 2 * kz
        self.ny = gz // 2 // NX
        self.light = 2 * self.ny
        self.heavy = NX * gy
        self.deep = rows // PIECES
        self.block = kx * self.deep


def tables_of(s):
    bx, by, bz = basis_table(s.kx, s.line), basis_table(s.ky, s.rows * s.gy), basis_table(s.kz, 2 * s.gz)
    bx = bx[np.arange(s.kx).reshape(NX, s.gy).T.reshape(-1)]
    byd = by.reshape(s.ky, s.gy, s.rows)
    ty = by.reshape(s.ky, s.gy, PIECES, s.deep).transpose(0, 2, 1, 3).reshape(s.ky, PIECES, s.gy * s.deep)
    bzg = bz.reshape(s.kz, s.ny, NX, 2, 2)
    two = np.eye(2, dtype=np.float32)
    tz = np.einsum("kyxaz,ij->izkyajx", bzg, two).reshape(4 * s.kz, 8 * s.light)
    tza = np.einsum("kyxaz,r->zkyaxr", bzg, np.eye(1, 2, dtype=np.float32)[0]).reshape(2 * s.kz, 8 * s.light)
    ma = np.zeros((s.gy, 2, 2, s.rows, s.ky, 2, 2), np.float32)
    for f in range(2):
        for z in range(2):
            ma[:, f, z, :, :, z, f] = byd.transpose(1, 2, 0)
    ma = ma.reshape(s.gy, 4 * s.rows, 4 * s.ky)
    full = np.zeros((s.gy, 128, 128), np.float32)
    full[:, : 4 * s.rows, : 4 * s.ky] = ma
    ym = np.broadcast_to(byd.transpose(1, 0, 2)[:, :, None, None, None, :], (s.gy, s.ky, NX, NX, 2, s.rows))
    ym = np.ascontiguousarray(ym).reshape(s.gy, s.ky * NX, NX * 2 * s.rows)
    txs = np.zeros((s.kx, 2, s.line), np.float32)
    txs[:, 0] = bx
    lanes = np.arange(256)
    expand = (np.arange(128)[None, :, None] % 64 == 4 * np.arange(16)[:, None, None] + lanes[None, None, :] // 64)
    return [
        bx,
        txs.reshape(2 * s.kx, s.line),
        wide(bx),
        wide(np.ascontiguousarray(bx.T)),
        np.stack([wide(ty[:, p]) for p in range(PIECES)]),
        wide(np.ascontiguousarray(ty.reshape(s.ky, -1).T)),
        wide(tz),
        wide(np.ascontiguousarray(tz.T)),
        tza,
        full,
        ym,
        expand.astype(ml_dtypes.bfloat16),
        np.concatenate([np.eye(64, dtype=np.float32)] * 2, axis=1),
    ]


def split(x):
    high = x.astype(jnp.bfloat16)
    return high, (x - high.astype(jnp.float32)).astype(jnp.bfloat16)


def tall3(x):
    high, low = split(x)
    return jnp.concatenate([high, high, low], axis=0)


def flat3(x):
    high, low = split(x)
    return jnp.concatenate([high, high, low], axis=1)


def dot(a, b):
    return jnp.dot(a, b, preferred_element_type=jnp.float32)


def gelu_parts(grid_field):
    normal_cdf = 0.5 * (1.0 + lax.erf(grid_field * (1.0 / math.sqrt(2.0))))
    density = jnp.exp(-0.5 * grid_field * grid_field) * (1.0 / math.sqrt(2.0 * math.pi))
    return (grid_field * normal_cdf, normal_cdf + grid_field * density)


def total(x):
    return jnp.sum(jnp.sum(x, axis=0, keepdims=True), axis=1, keepdims=True)


def kernel(s, *refs):
    (kappa, weight, rhs, gain_in, bias_in, b1_in, b2_in, read_in, l1_in, l2_in, tx, txk, tx3, txt3, tz3, tzt3, twice,
     w1_in, w2_in, ty3_in, tyt3_in, tza_in, ma_in, ym_in, expand_in,
     out,
     send_y, recv_y, send_z, recv_z, send_zs, recv_zs, send_s, recv_s,
     send_a, recv_a, send_az, recv_az, send_pz, recv_pz, send_py, recv_py,
     mats3, kb, rb, wb, slope_one, slope_two, act, tan, back, pred0, qb, lb, vecs, plane, gain_own, gain_new,
     w1, w2, ty3, tyt3, tza, ma, ym, expand,
     sy, ry, sz, rz, ss, rs, sa, ra, spz, rpz, spy, rpy, sw, rw, loads) = refs
    me_z, me_y = lax.axis_index("gz"), lax.axis_index("gy")
    core, chip = lax.rem(me_z, 2), lax.div(me_z, 2)
    at_y, at_x = lax.div(chip, NX), lax.rem(chip, NX)
    me_light, me_heavy = at_y * 2 + core, me_y * NX + at_x
    f32 = jnp.float32

    brought = {}
    for i, (src, dst) in enumerate(
        ((ma_in, ma), (expand_in, expand), (w1_in, w1), (tza_in, tza), (tyt3_in, tyt3), (ty3_in, ty3), (ym_in, ym))
    ):
        brought[id(dst)] = pltpu.make_async_copy(src, dst, loads.at[i])
        brought[id(dst)].start()

    def ready(dst):
        brought[id(dst)].wait()

    def place(y, x, c):
        return (y * NX + x) * 2 + c

    def far_first(*rings):
        steps = [()]
        for n in rings:
            steps = [step + (k,) for step in steps for k in range(n)]
        far = lambda step: -sum(min(k, n - k) for k, n in zip(step, rings))
        return sorted((step for step in steps if any(step)), key=far)

    heavy_steps, light_steps = far_first(s.gy, NX), far_first(s.ny, 2)

    def peers_heavy(visit):
        for dz, dx in heavy_steps:
            z, x = lax.rem(me_y + dz, s.gy), lax.rem(at_x + dx, NX)
            visit(z * NX + x, {"gz": place(at_y, x, core), "gy": z})

    def peers_light(visit):
        for dy, dc in light_steps:
            y, c = lax.rem(at_y + dy, s.ny), lax.rem(core + dc, 2)
            visit(y * 2 + c, {"gz": place(y, at_x, c)})

    new_core, new_slot = lax.div(at_x, 2), lax.rem(at_x, 2)
    movers = [(2 * core + j, place(at_y, 2 * core + j, new_core)) for j in range(2)]

    barrier = pltpu.get_barrier_semaphore()
    greet = lambda _, device: pl.semaphore_signal(barrier, inc=1, device_id=device, device_id_type=MESH)
    peers_heavy(greet)
    peers_light(greet)
    for dx in range(1, NX):
        greet(None, {"gz": place(at_y, lax.rem(at_x + dx, NX), 1 - core)})
    greeted = len(heavy_steps) + len(light_steps) + NX - 1

    def exchange_heavy(src_of, dst, send_sem, recv_sem):
        peers_heavy(
            lambda n, device: pltpu.make_async_remote_copy(
                src_of(n), dst, send_sem, recv_sem, device_id=device, device_id_type=MESH
            ).start()
        )
        pltpu.make_async_copy(src_of(me_heavy), dst, recv_sem).start()

    def exchange_light(src_of, dst, send_sem, recv_sem):
        peers_light(
            lambda n, device: pltpu.make_async_remote_copy(
                src_of(n), dst, send_sem, recv_sem, device_id=device, device_id_type=MESH
            ).start()
        )
        pltpu.make_async_copy(src_of(me_light), dst, recv_sem).start()

    def move(src_of, dst, send_sem, recv_sem):
        for j, (x, target) in enumerate(movers):
            @pl.when(target != me_z)
            def _():
                pltpu.make_async_remote_copy(
                    src_of(j), dst.at[new_slot], send_sem, recv_sem, device_id={"gz": target}, device_id_type=MESH
                ).start()

            @pl.when(target == me_z)
            def _():
                pltpu.make_async_copy(src_of(j), dst.at[new_slot], recv_sem).start()

    def left(src_of, send_sem):
        for j, (x, target) in enumerate(movers):
            @pl.when(target != me_z)
            def _():
                wait(src_of(j), send_sem)

    def wait(ref, sem):
        pltpu.make_async_copy(ref, ref, sem).wait()

    def piece(p):
        return slice(p * s.block, (p + 1) * s.block)

    def piece_gy(e, p):
        rows = lambda n: pl.ds(pl.multiple_of(p * s.block + n * s.deep, s.deep), s.deep)
        exchange_heavy(lambda n: send_y.at[e, rows(n)], recv_y.at[e, rows(me_heavy)], sy.at[e], ry.at[e, p])

    def wait_gy(e, p):
        wait(recv_y.at[e, pl.ds(p * s.block, s.block)], ry.at[e, p])

    def eight(n):
        return pl.ds(pl.multiple_of(n * 8, 8), 8)

    def unit_gz(e):
        if e in SUMS:
            i = SUMS[e]
            exchange_light(lambda n: send_zs.at[i, n], recv_zs.at[i, me_light], sz.at[e], rz.at[e])
        else:
            exchange_light(lambda n: send_z.at[e, eight(n)], recv_z.at[e, eight(me_light)], sz.at[e], rz.at[e])

    def wait_gz(e):
        if e in SUMS:
            wait(recv_zs.at[SUMS[e]], rz.at[e])
        else:
            wait(recv_z.at[e], rz.at[e])

    lane = lax.broadcasted_iota(jnp.int32, (1, 128), 1)
    low_half = (lane < 64).astype(f32)
    high_half = 1.0 - low_half

    both = jnp.concatenate([kappa[...], rhs[...], jnp.zeros((128 - 4 * s.rows, 128), f32)], axis=0)
    spectrum = lax.dot_general(tx[...], both, NT, precision=HIGHEST, preferred_element_type=f32)
    own = jnp.sum(rhs[...] * rhs[...], axis=0, keepdims=True)
    for k in range(s.kx):
        send_a[k, 0:1, :] = spectrum[k : k + 1]
        send_a[k, 1:2, :] = own
    vecs[...] = jnp.zeros_like(vecs)
    for i, ref in enumerate((gain_in, bias_in, b1_in, b2_in, read_in)):
        vecs[i : i + 1, :] = ref[...]
    exact = functools.partial(jnp.dot, precision=HIGHEST, preferred_element_type=f32)
    doubled = exact(vecs[...], twice[...])
    lifted = exact(exact(vecs[...], l1_in[...]), twice[...])
    gain_row, read_row, bias_two = doubled[0:1], doubled[4:5], doubled[3:4]
    lift_row, bias_one = lifted[0:1], lifted[1:2] + doubled[2:3]
    same = lax.div(lax.broadcasted_iota(jnp.int32, (128, 128), 0), 64) == lax.div(
        lax.broadcasted_iota(jnp.int32, (128, 128), 1), 64
    )
    only = lambda x: jnp.where(same, x, 0.0)
    column = lambda x: only(jnp.broadcast_to(x, (128, 128)).T)
    local_two = only(jnp.concatenate([exact(l2_in[...], twice[...])] * 2, axis=0))
    row = lax.broadcasted_iota(jnp.int32, (128, 128), 0)
    two_rows = jnp.where((row == 0) & (lane < 64) | (row == 1) & (lane >= 64), jnp.broadcast_to(lift_row, (128, 128)), 0.0)
    pl.semaphore_wait(barrier, greeted)
    exchange_heavy(lambda n: send_a.at[n], recv_a.at[me_heavy], sa.at[0], ra.at[0])

    for m, table in enumerate((local_two, local_two.T, column(read_row), column(lift_row), two_rows)):
        high, low = split(table)
        mats3[m, 0:128, :] = high
        mats3[m, 128:256, :] = low
        mats3[m, 256:384, :] = high
    mix_two, mix_back, read_mat, lift_mat = range(4)

    gain_mix = jnp.zeros((s.modes, 128), f32)
    bias_mix = jnp.zeros((8, 128), f32)
    high, low = split(doubled)
    packed = jnp.where(lane < 64, high.astype(f32), low.astype(f32)).astype(jnp.bfloat16)
    ready(expand)
    ready(w1)
    for t in range(16):
        spread_rows = dot(packed, expand[t])
        for u in range(2):
            at = (2 * t + u) * 128
            part = spread_rows[:, u * 128 : (u + 1) * 128]
            gain_mix = gain_mix + w1[:, at : at + 128] * part[0:1]
            bias_mix = bias_mix + w1[0:8, at : at + 128] * part[1:2]
    gain_own[...] = (gain_mix + pltpu.roll(gain_mix, 64, 1)).reshape(2, s.kz, 128)
    move(lambda j: gain_own.at[j], gain_new, sw.at[0], rw.at[0])
    move(lambda j: w2_in.at[j], w2, sw.at[1], rw.at[1])
    bias_mix = bias_mix + pltpu.roll(bias_mix, 64, 1)
    is_mean = ((me_z == 0) & (me_y == 0)).astype(f32)
    first_row = (lax.broadcasted_iota(jnp.int32, (8, 128), 0) == 0).astype(f32)
    volume = math.sqrt(float(2 * s.gz) * float(s.rows * s.gy) * float(s.line))
    bias_mix = bias_mix * first_row * (is_mean * volume)

    ready(ma)
    wait(recv_a, ra.at[0])
    mixed = jnp.zeros((8, 128), f32)
    own = jnp.zeros((8, 128), f32)
    for d in range(s.gy):
        rows = recv_a[d * NX : (d + 1) * NX].reshape(8, 128)
        mixed = mixed + jnp.dot(rows, ma[d], precision=HIGHEST, preferred_element_type=f32)
        own = own + rows
    odd = (lax.rem(lax.broadcasted_iota(jnp.int32, (8, 128), 0), 2) == 1)
    send_az[...] = jnp.where(odd, own, mixed)
    exchange_light(lambda n: send_az, recv_az.at[eight(me_light)], sa.at[1], ra.at[1])

    def spread(p, carry):
        for src, dst in ((kappa, kb), (rhs, rb), (weight, wb)):
            for y in range(s.deep):
                near = jnp.broadcast_to(src[pl.ds(p * s.deep + y, 1), :], (64, 128))
                far = jnp.broadcast_to(src[pl.ds(s.rows + p * s.deep + y, 1), :], (64, 128))
                dst[p, :, y * 128 : (y + 1) * 128] = jnp.concatenate([near, far], axis=0).T
        return carry

    lax.fori_loop(0, PIECES, spread, 0)

    ready(tza)
    wait(recv_az, ra.at[1])
    arrived = recv_az[...]
    row = lax.broadcasted_iota(jnp.int32, arrived.shape, 0)
    norm_zero = total(jnp.where(lax.rem(row, 2) == 1, arrived, 0.0))
    coeffs = jnp.dot(tza[...], arrived, precision=HIGHEST, preferred_element_type=f32)

    def pick(f):
        columns = []
        for j in range(2):
            kept = jnp.zeros((s.kz, 128), f32)
            for z in range(2):
                at = (4 * at_y + 2 * core + j) * 4 + z * 2 + f
                kept = kept + coeffs[z * s.kz : (z + 1) * s.kz] * (lane == at).astype(f32)
            columns.append(jnp.sum(kept, axis=1, keepdims=True))
        return jnp.concatenate(columns, axis=0)

    modes_kappa, modes_rhs = pick(0), pick(1)
    wait(gain_new, rw.at[0])
    gain_mix = gain_new[...].reshape(s.modes, 128)

    def cells_z(e, values):
        pieces = []
        for j in range(2):
            half = values[j * s.kz : (j + 1) * s.kz]
            pieces += [half * low_half, half * high_half]
        send_z[e] = dot(tzt3[...], tall3(jnp.concatenate(pieces, axis=0)))
        unit_gz(e)

    def groups(ref, *at):
        return jnp.concatenate([ref[(*at, pl.ds(x, s.ky, stride=NX), slice(None))] for x in range(NX)], axis=1)

    def cells_y(e):
        wait_gz(e)
        values = tall3(groups(recv_z, e))
        half = s.gy * s.deep
        for p in range(PIECES):
            sent = dot(tyt3[p * half : (p + 1) * half, :], values)
            for d in range(s.gy):
                for x in range(NX):
                    at = p * s.block + (d * NX + x) * s.deep
                    send_y[e, at : at + s.deep, :] = sent[d * s.deep : (d + 1) * s.deep, x * 128 : (x + 1) * 128]
            piece_gy(e, p)

    def cells_x(e, p):
        wait_gy(e, p)
        rows = [recv_y[e, pl.ds(p * s.block + y, s.kx, stride=s.deep), :] for y in range(s.deep)]
        return dot(txt3[...], tall3(jnp.concatenate(rows, axis=1)))

    def modes_x(e, p, parts):
        high, low = parts
        sent = dot(tx3[...], jnp.concatenate([high, high, low], axis=0))
        for y in range(s.deep):
            send_y[e, pl.ds(p * s.block + y, s.kx, stride=s.deep), :] = sent[:, y * 128 : (y + 1) * 128]
        piece_gy(e, p)

    def modes_sum(e, partial):
        i = SUMS[e]
        send_s[i] = jnp.broadcast_to(partial, (2, 128))
        exchange_heavy(lambda n: send_s.at[i], recv_s.at[i, me_heavy], ss.at[i], rs.at[i])

    def modes_y(e):
        sent = jnp.zeros((s.ky, NX * 128), f32)
        for p in range(PIECES):
            wait_gy(e, p)
            field = []
            for x in range(NX):
                at = [p * s.block + (d * NX + x) * s.deep for d in range(s.gy)]
                field.append(jnp.concatenate([recv_y[e, a : a + s.deep, :] for a in at], axis=0))
            sent = sent + dot(ty3[p], tall3(jnp.concatenate(field, axis=1)))
        for x in range(NX):
            send_z[e, pl.ds(x, s.ky, stride=NX), :] = sent[:, x * 128 : (x + 1) * 128]
        if e in SUMS:
            i = SUMS[e]
            wait(recv_s.at[i], rs.at[i])
            partial = jnp.sum(recv_s[i].reshape(2 * s.heavy, 128), axis=0, keepdims=True) * 0.5
            send_zs[i, :, 0:8, :] = send_z[e].reshape(s.light, 8, 128)
            send_zs[i, :, 8:16, :] = jnp.broadcast_to(partial[None], (s.light, 8, 128))
        unit_gz(e)

    def modes_z(e):
        wait_gz(e)
        summed = None
        if e in SUMS:
            i = SUMS[e]
            arrived = recv_zs[i, :, 0:8, :].reshape(8 * s.light, 128)
            summed = total(recv_zs[i, :, 8:9, :].reshape(s.light, 128))
        else:
            arrived = recv_z[e]
        coeffs = dot(tz3[...], tall3(arrived))
        pieces = []
        for j in range(2):
            at = 2 * j * s.kz
            pieces.append(coeffs[at : at + s.kz] * low_half + coeffs[at + s.kz : at + 2 * s.kz] * high_half)
        values = jnp.concatenate(pieces, axis=0)
        return values + pltpu.roll(values, 64, 1), summed

    def mix_forward(values):
        high, low = split(values)
        low_lanes = lane < 64
        packed = jnp.where(low_lanes, high.astype(f32), low.astype(f32)).astype(jnp.bfloat16)
        mixed = jnp.zeros_like(values)
        mixed = jnp.zeros((s.modes, 256), f32)
        for t in range(16):
            mixed = mixed + dot(packed, expand[t]) * w2[:, :, t * 256 : (t + 1) * 256].reshape(s.modes, 256)
        mixed = mixed[:, :128] + mixed[:, 128:]
        return mixed + pltpu.roll(mixed, 64, 1)

    def mix_adjoint(values):
        mixed = jnp.zeros((2 * s.modes, 128), f32)
        values = jnp.concatenate([values, values], axis=1)
        for t in range(16):
            high, low = split(values * w2[:, :, t * 256 : (t + 1) * 256].reshape(s.modes, 256))
            packed = jnp.concatenate([high, low], axis=0)
            mixed = mixed + lax.dot_general(packed, expand[t], NT, preferred_element_type=f32)
        return mixed[: s.modes] + mixed[s.modes :]

    def scalar_z(i, coeffs):
        pieces = []
        for j in range(2):
            for z in range(2):
                mask = (lax.rem(lax.div(lane, s.rows), 2) == z).astype(f32)
                pieces.append(coeffs[j * s.kz : (j + 1) * s.kz] * mask)
        sent = dot(tzt3[...], tall3(jnp.concatenate(pieces, axis=0)))
        row = lax.broadcasted_iota(jnp.int32, sent.shape, 0)
        send_pz[i] = jnp.where(lax.rem(row, NX) == lax.div(lane, 2 * s.rows), sent, 0.0)
        exchange_light(lambda n: send_pz.at[i, eight(n)], recv_pz.at[i, eight(me_light)], spz.at[i], rpz.at[i])

    def scalar_y(i):
        wait(recv_pz.at[i], rpz.at[i])
        arrived = recv_pz[i]
        for d in range(s.gy):
            summed = jnp.sum(arrived * ym[d], axis=0, keepdims=True)
            send_py[i, d] = jnp.broadcast_to(summed, (2, 128))
        exchange_heavy(
            lambda n: send_py.at[i, lax.div(n, NX)], recv_py.at[i, me_heavy], spy.at[i], rpy.at[i]
        )

    def scalar_x(i):
        wait(recv_py.at[i], rpy.at[i])
        columns = recv_py[i].reshape(2 * s.heavy, 128).T
        plane[...] = jnp.dot(columns, txk[...], precision=HIGHEST, preferred_element_type=f32)
        return plane[pl.ds(pl.multiple_of(at_x * 2 * s.rows, 2 * s.rows), 2 * s.rows), :]

    def lines(x):
        return jnp.concatenate([x[:, y * 128 : (y + 1) * 128] for y in range(s.deep)], axis=0)

    def across(x):
        return jnp.concatenate([x[y * 128 : (y + 1) * 128] for y in range(s.deep)], axis=1)

    def mat(m, parts):
        high, low = lines(parts[0]), lines(parts[1])
        return across(dot(jnp.concatenate([high, high, low], axis=1), mats3[m]))

    def fold(x):
        x = jnp.sum(x, axis=0, keepdims=True)
        return sum(x[:, y * 128 : (y + 1) * 128] for y in range(s.deep))

    def local_rows(i, p, parts):
        high, low = lines(parts[0]), lines(parts[1])
        rows = lax.dot_general(mats3[4, 0:16, :], high, NT, preferred_element_type=f32)
        rows = rows + lax.dot_general(mats3[4, 128:144, :], high, NT, preferred_element_type=f32)
        rows = rows + lax.dot_general(mats3[4, 0:16, :], low, NT, preferred_element_type=f32)
        for y in range(s.deep):
            lb[i, p * s.deep + y : p * s.deep + y + 1, :] = rows[0:1, y * 128 : (y + 1) * 128]
            at = s.rows + p * s.deep + y
            lb[i, at : at + 1, :] = rows[1:2, y * 128 : (y + 1) * 128]

    wide_row = lambda x: jnp.concatenate([x] * s.deep, axis=1)
    lift_wide, one_wide, two_wide, read_wide = map(wide_row, (lift_row, bias_one, bias_two, read_row))
    empty = jnp.zeros((1, 128), f32)

    values = modes_kappa * gain_mix
    cells_z(B0K, jnp.concatenate([values[0:8] + bias_mix, values[8:]], axis=0))
    cells_z(B0R, modes_rhs * gain_mix)
    ready(tyt3)
    cells_y(B0K)
    cells_y(B0R)
    for p in range(PIECES):
        value, slope = gelu_parts(cells_x(B0K, p) + lift_wide * kb[p] + one_wide)
        act[p] = value
        slope_one[p] = slope
        modes_x(C0A, p, split(value))
    for p in range(PIECES):
        value = slope_one[p] * (cells_x(B0R, p) + lift_wide * rb[p])
        tan[p] = value
        modes_x(C0T, p, split(value))
    ready(ty3)
    modes_y(C0A)
    modes_y(C0T)
    wait(w2, rw.at[1])
    values, _ = modes_z(C0A)
    cells_z(D0A, mix_forward(values))
    values, _ = modes_z(C0T)
    cells_z(D0T, mix_forward(values))
    cells_y(D0A)
    cells_y(D0T)
    for p in range(PIECES):
        _, slope = gelu_parts(cells_x(D0A, p) + mat(mix_two, split(act[p])) + two_wide)
        slope_two[p] = slope
    norms = empty
    for p in range(PIECES):
        slope = slope_two[p]
        tangent = slope * (cells_x(D0T, p) + mat(mix_two, split(tan[p])))
        predicted = mat(read_mat, split(tangent))
        pred0[p] = predicted
        weighted = wb[p] * predicted
        value = slope * (read_wide * weighted)
        back[p] = value
        modes_x(E0, p, split(value))
        norms = norms + fold(weighted * predicted)
    modes_sum(E0, norms)
    modes_y(E0)
    values, curvature = modes_z(E0)
    curvature = curvature * (1.0 / 64.0) + DAMPING * norm_zero
    step_zero = norm_zero / curvature
    cells_z(F0, mix_adjoint(values))
    cells_y(F0)
    for p in range(PIECES):
        value = slope_one[p] * (cells_x(F0, p) + mat(mix_back, split(back[p])))
        parts = split(value)
        modes_x(G0, p, parts)
        local_rows(0, p, parts)
        qb[p] = rb[p] * (1.0 - DAMPING * step_zero) - step_zero * mat(lift_mat, parts)
    modes_y(G0)
    values, _ = modes_z(G0)

    coeffs_zero = jnp.sum(values * gain_mix * low_half, axis=1, keepdims=True)
    image = coeffs_zero + jnp.sum(values * lift_row * low_half, axis=1, keepdims=True) + DAMPING * modes_rhs
    modes_res = modes_rhs - step_zero * image
    cells_z(B1, modes_res * gain_mix - (step_zero * coeffs_zero) * lift_row)
    scalar_z(0, coeffs_zero)
    cells_y(B1)
    ready(ym)
    scalar_y(0)
    for p in range(PIECES):
        value = slope_one[p] * (cells_x(B1, p) + lift_wide * qb[p])
        tan[p] = value
        modes_x(C1, p, split(value))
    right = rhs[...]
    applied_zero = scalar_x(0) + lb[0] + DAMPING * right
    residual = right - step_zero * applied_zero
    modes_sum(C1, jnp.sum(residual * residual, axis=0, keepdims=True))
    modes_y(C1)
    values, norm_one = modes_z(C1)
    cells_z(D1, mix_forward(values))
    ratio = norm_one / norm_zero
    direction = residual + ratio * right
    cells_y(D1)
    norms = empty
    for p in range(PIECES):
        slope = slope_two[p]
        tangent = slope * (cells_x(D1, p) + mat(mix_two, split(tan[p])))
        predicted = mat(read_mat, split(tangent))
        value = slope * (read_wide * (wb[p] * predicted))
        back[p] = value
        modes_x(E1, p, split(value))
        moved = predicted + ratio * pred0[p]
        norms = norms + fold(wb[p] * moved * moved)
    norms = norms * (1.0 / 64.0) + DAMPING * jnp.sum(direction * direction, axis=0, keepdims=True)
    modes_sum(E1, norms)
    modes_y(E1)
    values, curvature = modes_z(E1)
    step_one = norm_one / curvature
    cells_z(F1, mix_adjoint(values))
    cells_y(F1)
    for p in range(PIECES):
        value = slope_one[p] * (cells_x(F1, p) + mat(mix_back, split(back[p])))
        parts = split(value)
        modes_x(G1, p, parts)
        local_rows(1, p, parts)
    modes_y(G1)
    values, _ = modes_z(G1)
    scalar_z(1, jnp.sum(values * gain_mix * low_half, axis=1, keepdims=True))
    scalar_y(1)
    applied = scalar_x(1) + lb[1] + DAMPING * residual + ratio * applied_zero
    out[0] = step_zero * right + step_one * direction
    out[1] = residual - step_one * applied

    for e in range(UNITS):
        wait(send_y.at[e, pl.ds(0, s.rows * (s.heavy - 1))], sy.at[e])
        if e in SUMS:
            wait(send_zs.at[SUMS[e], pl.ds(0, s.light - 1)], sz.at[e])
        else:
            wait(send_z.at[e, pl.ds(0, 8 * (s.light - 1))], sz.at[e])
    for i in range(3):
        wait(recv_s.at[i, pl.ds(0, s.heavy - 1)], ss.at[i])
    wait(send_a.at[pl.ds(0, s.heavy - 1)], sa.at[0])
    wait(recv_az.at[pl.ds(0, 8 * (s.light - 1))], sa.at[1])
    for i in range(2):
        wait(send_pz.at[i, pl.ds(0, 8 * (s.light - 1))], spz.at[i])
        wait(recv_py.at[i, pl.ds(0, s.heavy - 1)], spy.at[i])
    left(lambda j: gain_own.at[j], sw.at[0])
    left(lambda j: w2_in.at[j], sw.at[1])


def local(
    s,
    log_kappa,
    misfit_weight,
    right_side,
    lift_gain,
    lift_bias,
    spec_one,
    spec_two,
    local_one,
    local_two,
    bias_one,
    bias_two,
    readout,
):
    shape = log_kappa.shape
    rows = lambda x: x.reshape(2 * s.rows, s.line)
    row = lambda x: x.reshape(1, 64)
    tables = [jnp.asarray(t) for t in tables_of(s)]
    tx, txk, tx3, txt3, ty3, tyt3, tz3, tzt3, tza, ma, ym, expand, twice = tables
    near = [
        rows(log_kappa), rows(misfit_weight), rows(right_side),
        row(lift_gain), row(lift_bias), row(bias_one), row(bias_two), row(readout),
        local_one, local_two, tx, txk, tx3, txt3, tz3, tzt3, twice,
    ]
    far = [spec_one.reshape(s.modes, 4096), spec_two.reshape(2, s.kz, 4096), ty3, tyt3, tza, ma, ym, expand]
    f32, bf16 = jnp.float32, jnp.bfloat16
    vmem = lambda *dims: pltpu.VMEM(dims, f32)
    half = s.kx * s.rows
    cell = (PIECES, 128, 128 * s.deep)
    scratch = [
        vmem(UNITS, half, 128), vmem(UNITS, half, 128),
        vmem(UNITS, 8 * s.light, 128), vmem(UNITS, 8 * s.light, 128),
        vmem(3, s.light, 16, 128), vmem(3, s.light, 16, 128),
        vmem(3, 2, 128), vmem(3, s.heavy, 2, 128),
        vmem(s.heavy, 2, 128), vmem(s.heavy, 2, 128),
        vmem(8, 128), vmem(8 * s.light, 128),
        vmem(2, 8 * s.light, 128), vmem(2, 8 * s.light, 128),
        vmem(2, s.gy, 2, 128), vmem(2, s.heavy, 2, 128),
        pltpu.VMEM((5, 384, 128), bf16),
    ] + [vmem(*cell) for _ in range(10)] + [vmem(2, 2 * s.rows, 128), vmem(8, 64), vmem(128, 128)]
    scratch += [vmem(2, s.kz, 128), vmem(2, s.kz, 128)]
    scratch += [pltpu.VMEM(x.shape, x.dtype) for x in far]
    counts = [(UNITS,), (UNITS, PIECES), (UNITS,), (UNITS,), (3,), (3,), (2,), (2,), (2,), (2,), (2,), (2,), (2,), (2,), (len(far),)]
    scratch += [pltpu.SemaphoreType.DMA(n) for n in counts]
    result = pl.pallas_call(
        functools.partial(kernel, s),
        out_shape=jax.ShapeDtypeStruct((2, 2 * s.rows, s.line), f32),
        in_specs=[pl.BlockSpec(memory_space=pltpu.VMEM)] * len(near) + [pl.BlockSpec(memory_space=pl.ANY)] * len(far),
        out_specs=pl.BlockSpec(memory_space=pltpu.VMEM),
        scratch_shapes=scratch,
        compiler_params=pltpu.CompilerParams(
            collective_id=0, has_side_effects=True, vmem_limit_bytes=60 * 1024 * 1024
        ),
        name="two_steps",
    )(*near, *far)
    return tuple(result[i].reshape(shape) for i in range(2))


def solution(mesh, kx=KX, ky=KY, kz=KZ, rows=16, line=128):
    s = Sizes(mesh.shape["gz"], mesh.shape["gy"], rows, line, kx, ky, kz)
    field = P("gz", "gy", None)
    weights = P("gz", "gy", None, None)
    return jax.shard_map(
        functools.partial(local, s),
        mesh=mesh,
        in_specs=(field, field, field, P(), P(), weights, weights, P(), P(), P(), P(), P()),
        out_specs=(field, field),
        check_vma=False,
    )
```

```python
import functools
import math

import jax
import jax.numpy as jnp
import ml_dtypes
import numpy as np
from jax import lax
from jax.experimental import pallas as pl
from jax.experimental.pallas import tpu as pltpu
from jax.sharding import PartitionSpec as P

KX = 32
KY = 32
KZ = 32
DAMPING = 0.3
HIGHEST = lax.Precision.HIGHEST
MESH = pl.DeviceIdType.MESH
NT = (((1,), (1,)), ((), ()))
UNITS = 15
B0K, B0R, C0A, C0T, D0A, D0T, E0, F0, G0, B1, C1, D1, E1, F1, G1 = range(UNITS)
SUMS = {E0: 0, C1: 1, E1: 2}
PIECES = 4
NX = 4


def basis_table(modes, length):
    mode_index = np.arange(modes)
    frequency = (mode_index + 1) // 2
    phase_steps = frequency[:, None] * np.arange(length)[None, :] % length
    angles = phase_steps * (2.0 * math.pi / length)
    is_sine = (mode_index % 2 == 0) & (mode_index > 0)
    scales = np.where(mode_index == 0, math.sqrt(1.0 / length), math.sqrt(2.0 / length))
    return (np.where(is_sine[:, None], np.sin(angles), np.cos(angles)) * scales[:, None]).astype(np.float32)


def parts_of(table):
    high = table.astype(ml_dtypes.bfloat16)
    low = (table - high.astype(np.float32)).astype(ml_dtypes.bfloat16)
    return high, low


def wide(table):
    high, low = parts_of(table)
    return np.concatenate([high, low, high], axis=1)


class Sizes:
    def __init__(self, gz, gy, rows, line, kx, ky, kz):
        self.gz, self.gy, self.rows, self.line = gz, gy, rows, line
        self.kx, self.ky, self.kz = kx, ky, kz
        self.modes = 2 * kz
        self.ny = gz // 2 // NX
        self.light = 2 * self.ny
        self.heavy = NX * gy
        self.deep = rows // PIECES
        self.block = kx * self.deep


def tables_of(s):
    bx, by, bz = basis_table(s.kx, s.line), basis_table(s.ky, s.rows * s.gy), basis_table(s.kz, 2 * s.gz)
    bx = bx[np.arange(s.kx).reshape(NX, s.gy).T.reshape(-1)]
    byd = by.reshape(s.ky, s.gy, s.rows)
    ty = by.reshape(s.ky, s.gy, PIECES, s.deep).transpose(0, 2, 1, 3).reshape(s.ky, PIECES, s.gy * s.deep)
    bzg = bz.reshape(s.kz, s.ny, NX, 2, 2)
    two = np.eye(2, dtype=np.float32)
    tz = np.einsum("kyxaz,ij->izkyajx", bzg, two).reshape(4 * s.kz, 8 * s.light)
    tza = np.einsum("kyxaz,r->zkyaxr", bzg, np.eye(1, 2, dtype=np.float32)[0]).reshape(2 * s.kz, 8 * s.light)
    ma = np.zeros((s.gy, 2, 2, s.rows, s.ky, 2, 2), np.float32)
    for f in range(2):
        for z in range(2):
            ma[:, f, z, :, :, z, f] = byd.transpose(1, 2, 0)
    ma = ma.reshape(s.gy, 4 * s.rows, 4 * s.ky)
    full = np.zeros((s.gy, 128, 128), np.float32)
    full[:, : 4 * s.rows, : 4 * s.ky] = ma
    ym = np.broadcast_to(byd.transpose(1, 0, 2)[:, :, None, None, None, :], (s.gy, s.ky, NX, NX, 2, s.rows))
    ym = np.ascontiguousarray(ym).reshape(s.gy, s.ky * NX, NX * 2 * s.rows)
    txs = np.zeros((s.kx, 2, s.line), np.float32)
    txs[:, 0] = bx
    lanes = np.arange(256)
    expand = (np.arange(128)[None, :, None] % 64 == 4 * np.arange(16)[:, None, None] + lanes[None, None, :] // 64)
    return [
        bx,
        txs.reshape(2 * s.kx, s.line),
        wide(bx),
        wide(np.ascontiguousarray(bx.T)),
        np.stack([wide(ty[:, p]) for p in range(PIECES)]),
        wide(np.ascontiguousarray(ty.reshape(s.ky, -1).T)),
        wide(tz),
        wide(np.ascontiguousarray(tz.T)),
        tza,
        full,
        ym,
        expand.astype(ml_dtypes.bfloat16),
        np.concatenate([np.eye(64, dtype=np.float32)] * 2, axis=1),
    ]


def split(x):
    high = x.astype(jnp.bfloat16)
    return high, (x - high.astype(jnp.float32)).astype(jnp.bfloat16)


def tall3(x):
    high, low = split(x)
    return jnp.concatenate([high, high, low], axis=0)


def flat3(x):
    high, low = split(x)
    return jnp.concatenate([high, high, low], axis=1)


def dot(a, b):
    return jnp.dot(a, b, preferred_element_type=jnp.float32)


def gelu_parts(grid_field):
    normal_cdf = 0.5 * (1.0 + lax.erf(grid_field * (1.0 / math.sqrt(2.0))))
    density = jnp.exp(-0.5 * grid_field * grid_field) * (1.0 / math.sqrt(2.0 * math.pi))
    return (grid_field * normal_cdf, normal_cdf + grid_field * density)


def total(x):
    return jnp.sum(jnp.sum(x, axis=0, keepdims=True), axis=1, keepdims=True)


def kernel(s, *refs):
    (kappa, weight, rhs, gain_in, bias_in, b1_in, b2_in, read_in, l1_in, l2_in, tx, txk, tx3, txt3, tz3, tzt3, twice,
     w1_in, w2_in, ty3_in, tyt3_in, tza_in, ma_in, ym_in, expand_in,
     out,
     send_y, recv_y, send_z, recv_z, send_zs, recv_zs, send_s, recv_s,
     send_a, recv_a, send_az, recv_az, send_pz, recv_pz, send_py, recv_py,
     mats3, kb, rb, wb, slope_one, slope_two, act, tan, back, pred0, qb, lb, vecs, plane, gain_own, gain_new,
     w1, w2, ty3, tyt3, tza, ma, ym, expand,
     sy, ry, sz, rz, ss, rs, sa, ra, spz, rpz, spy, rpy, sw, rw, loads) = refs
    me_z, me_y = lax.axis_index("gz"), lax.axis_index("gy")
    core, chip = lax.rem(me_z, 2), lax.div(me_z, 2)
    at_y, at_x = lax.div(chip, NX), lax.rem(chip, NX)
    me_light, me_heavy = at_y * 2 + core, me_y * NX + at_x
    f32 = jnp.float32

    brought = {}
    for i, (src, dst) in enumerate(
        ((ma_in, ma), (expand_in, expand), (w1_in, w1), (tza_in, tza), (tyt3_in, tyt3), (ty3_in, ty3), (ym_in, ym))
    ):
        brought[id(dst)] = pltpu.make_async_copy(src, dst, loads.at[i])
        brought[id(dst)].start()

    def ready(dst):
        brought[id(dst)].wait()

    def place(y, x, c):
        return (y * NX + x) * 2 + c

    def far_first(*rings):
        steps = [()]
        for n in rings:
            steps = [step + (k,) for step in steps for k in range(n)]
        far = lambda step: -sum(min(k, n - k) for k, n in zip(step, rings))
        return sorted((step for step in steps if any(step)), key=far)

    heavy_steps, light_steps = far_first(s.gy, NX), far_first(s.ny, 2)

    def peers_heavy(visit):
        for dz, dx in heavy_steps:
            z, x = lax.rem(me_y + dz, s.gy), lax.rem(at_x + dx, NX)
            visit(z * NX + x, {"gz": place(at_y, x, core), "gy": z})

    def peers_light(visit):
        for dy, dc in light_steps:
            y, c = lax.rem(at_y + dy, s.ny), lax.rem(core + dc, 2)
            visit(y * 2 + c, {"gz": place(y, at_x, c)})

    new_core, new_slot = lax.div(at_x, 2), lax.rem(at_x, 2)
    movers = [(2 * core + j, place(at_y, 2 * core + j, new_core)) for j in range(2)]

    barrier = pltpu.get_barrier_semaphore()
    greet = lambda _, device: pl.semaphore_signal(barrier, inc=1, device_id=device, device_id_type=MESH)
    peers_heavy(greet)
    peers_light(greet)
    for dx in range(1, NX):
        greet(None, {"gz": place(at_y, lax.rem(at_x + dx, NX), 1 - core)})
    greeted = len(heavy_steps) + len(light_steps) + NX - 1

    def exchange_heavy(src_of, dst, send_sem, recv_sem):
        peers_heavy(
            lambda n, device: pltpu.make_async_remote_copy(
                src_of(n), dst, send_sem, recv_sem, device_id=device, device_id_type=MESH
            ).start()
        )
        pltpu.make_async_copy(src_of(me_heavy), dst, recv_sem).start()

    def exchange_light(src_of, dst, send_sem, recv_sem):
        peers_light(
            lambda n, device: pltpu.make_async_remote_copy(
                src_of(n), dst, send_sem, recv_sem, device_id=device, device_id_type=MESH
            ).start()
        )
        pltpu.make_async_copy(src_of(me_light), dst, recv_sem).start()

    def move(src_of, dst, send_sem, recv_sem):
        for j, (x, target) in enumerate(movers):
            @pl.when(target != me_z)
            def _():
                pltpu.make_async_remote_copy(
                    src_of(j), dst.at[new_slot], send_sem, recv_sem, device_id={"gz": target}, device_id_type=MESH
                ).start()

            @pl.when(target == me_z)
            def _():
                pltpu.make_async_copy(src_of(j), dst.at[new_slot], recv_sem).start()

    def left(src_of, send_sem):
        for j, (x, target) in enumerate(movers):
            @pl.when(target != me_z)
            def _():
                wait(src_of(j), send_sem)

    def wait(ref, sem):
        pltpu.make_async_copy(ref, ref, sem).wait()

    def piece(p):
        return slice(p * s.block, (p + 1) * s.block)

    def piece_gy(e, p):
        rows = lambda n: pl.ds(pl.multiple_of(p * s.block + n * s.deep, s.deep), s.deep)
        exchange_heavy(lambda n: send_y.at[e, rows(n)], recv_y.at[e, rows(me_heavy)], sy.at[e], ry.at[e, p])

    def wait_gy(e, p):
        wait(recv_y.at[e, pl.ds(p * s.block, s.block)], ry.at[e, p])

    def eight(n):
        return pl.ds(pl.multiple_of(n * 8, 8), 8)

    def unit_gz(e):
        if e in SUMS:
            i = SUMS[e]
            exchange_light(lambda n: send_zs.at[i, n], recv_zs.at[i, me_light], sz.at[e], rz.at[e])
        else:
            exchange_light(lambda n: send_z.at[e, eight(n)], recv_z.at[e, eight(me_light)], sz.at[e], rz.at[e])

    def wait_gz(e):
        if e in SUMS:
            wait(recv_zs.at[SUMS[e]], rz.at[e])
        else:
            wait(recv_z.at[e], rz.at[e])

    lane = lax.broadcasted_iota(jnp.int32, (1, 128), 1)
    low_half = (lane < 64).astype(f32)
    high_half = 1.0 - low_half

    both = jnp.concatenate([kappa[...], rhs[...], jnp.zeros((128 - 4 * s.rows, 128), f32)], axis=0)
    spectrum = lax.dot_general(tx[...], both, NT, precision=HIGHEST, preferred_element_type=f32)
    own = jnp.sum(rhs[...] * rhs[...], axis=0, keepdims=True)
    for k in range(s.kx):
        send_a[k, 0:1, :] = spectrum[k : k + 1]
        send_a[k, 1:2, :] = own
    vecs[...] = jnp.zeros_like(vecs)
    for i, ref in enumerate((gain_in, bias_in, b1_in, b2_in, read_in)):
        vecs[i : i + 1, :] = ref[...]
    exact = functools.partial(jnp.dot, precision=HIGHEST, preferred_element_type=f32)
    doubled = exact(vecs[...], twice[...])
    lifted = exact(exact(vecs[...], l1_in[...]), twice[...])
    gain_row, read_row, bias_two = doubled[0:1], doubled[4:5], doubled[3:4]
    lift_row, bias_one = lifted[0:1], lifted[1:2] + doubled[2:3]
    same = lax.div(lax.broadcasted_iota(jnp.int32, (128, 128), 0), 64) == lax.div(
        lax.broadcasted_iota(jnp.int32, (128, 128), 1), 64
    )
    only = lambda x: jnp.where(same, x, 0.0)
    column = lambda x: only(jnp.broadcast_to(x, (128, 128)).T)
    local_two = only(jnp.concatenate([exact(l2_in[...], twice[...])] * 2, axis=0))
    row = lax.broadcasted_iota(jnp.int32, (128, 128), 0)
    two_rows = jnp.where((row == 0) & (lane < 64) | (row == 1) & (lane >= 64), jnp.broadcast_to(lift_row, (128, 128)), 0.0)
    pl.semaphore_wait(barrier, greeted)
    exchange_heavy(lambda n: send_a.at[n], recv_a.at[me_heavy], sa.at[0], ra.at[0])

    for m, table in enumerate((local_two, local_two.T, column(read_row), column(lift_row), two_rows)):
        high, low = split(table)
        mats3[m, 0:128, :] = high
        mats3[m, 128:256, :] = low
        mats3[m, 256:384, :] = high
    mix_two, mix_back, read_mat, lift_mat = range(4)

    gain_mix = jnp.zeros((s.modes, 128), f32)
    bias_mix = jnp.zeros((8, 128), f32)
    high, low = split(doubled)
    packed = jnp.where(lane < 64, high.astype(f32), low.astype(f32)).astype(jnp.bfloat16)
    ready(expand)
    ready(w1)
    for t in range(16):
        spread_rows = dot(packed, expand[t])
        for u in range(2):
            at = (2 * t + u) * 128
            part = spread_rows[:, u * 128 : (u + 1) * 128]
            gain_mix = gain_mix + w1[:, at : at + 128] * part[0:1]
            bias_mix = bias_mix + w1[0:8, at : at + 128] * part[1:2]
    gain_own[...] = (gain_mix + pltpu.roll(gain_mix, 64, 1)).reshape(2, s.kz, 128)
    move(lambda j: gain_own.at[j], gain_new, sw.at[0], rw.at[0])
    move(lambda j: w2_in.at[j], w2, sw.at[1], rw.at[1])
    bias_mix = bias_mix + pltpu.roll(bias_mix, 64, 1)
    is_mean = ((me_z == 0) & (me_y == 0)).astype(f32)
    first_row = (lax.broadcasted_iota(jnp.int32, (8, 128), 0) == 0).astype(f32)
    volume = math.sqrt(float(2 * s.gz) * float(s.rows * s.gy) * float(s.line))
    bias_mix = bias_mix * first_row * (is_mean * volume)

    ready(ma)
    wait(recv_a, ra.at[0])
    mixed = jnp.zeros((8, 128), f32)
    own = jnp.zeros((8, 128), f32)
    for d in range(s.gy):
        rows = recv_a[d * NX : (d + 1) * NX].reshape(8, 128)
        mixed = mixed + jnp.dot(rows, ma[d], precision=HIGHEST, preferred_element_type=f32)
        own = own + rows
    odd = (lax.rem(lax.broadcasted_iota(jnp.int32, (8, 128), 0), 2) == 1)
    send_az[...] = jnp.where(odd, own, mixed)
    exchange_light(lambda n: send_az, recv_az.at[eight(me_light)], sa.at[1], ra.at[1])

    def spread(p, carry):
        for src, dst in ((kappa, kb), (rhs, rb), (weight, wb)):
            for y in range(s.deep):
                near = jnp.broadcast_to(src[pl.ds(p * s.deep + y, 1), :], (64, 128))
                far = jnp.broadcast_to(src[pl.ds(s.rows + p * s.deep + y, 1), :], (64, 128))
                dst[p, :, y * 128 : (y + 1) * 128] = jnp.concatenate([near, far], axis=0).T
        return carry

    lax.fori_loop(0, PIECES, spread, 0)

    ready(tza)
    wait(recv_az, ra.at[1])
    arrived = recv_az[...]
    row = lax.broadcasted_iota(jnp.int32, arrived.shape, 0)
    norm_zero = total(jnp.where(lax.rem(row, 2) == 1, arrived, 0.0))
    coeffs = jnp.dot(tza[...], arrived, precision=HIGHEST, preferred_element_type=f32)

    def pick(f):
        columns = []
        for j in range(2):
            kept = jnp.zeros((s.kz, 128), f32)
            for z in range(2):
                at = (4 * at_y + 2 * core + j) * 4 + z * 2 + f
                kept = kept + coeffs[z * s.kz : (z + 1) * s.kz] * (lane == at).astype(f32)
            columns.append(jnp.sum(kept, axis=1, keepdims=True))
        return jnp.concatenate(columns, axis=0)

    modes_kappa, modes_rhs = pick(0), pick(1)
    wait(gain_new, rw.at[0])
    gain_mix = gain_new[...].reshape(s.modes, 128)

    def cells_z(e, values):
        pieces = []
        for j in range(2):
            half = values[j * s.kz : (j + 1) * s.kz]
            pieces += [half * low_half, half * high_half]
        send_z[e] = dot(tzt3[...], tall3(jnp.concatenate(pieces, axis=0)))
        unit_gz(e)

    def groups(ref, *at):
        return jnp.concatenate([ref[(*at, pl.ds(x, s.ky, stride=NX), slice(None))] for x in range(NX)], axis=1)

    def cells_y(e):
        wait_gz(e)
        values = tall3(groups(recv_z, e))
        half = s.gy * s.deep
        for p in range(PIECES):
            sent = dot(tyt3[p * half : (p + 1) * half, :], values)
            for d in range(s.gy):
                for x in range(NX):
                    at = p * s.block + (d * NX + x) * s.deep
                    send_y[e, at : at + s.deep, :] = sent[d * s.deep : (d + 1) * s.deep, x * 128 : (x + 1) * 128]
            piece_gy(e, p)

    def cells_x(e, p):
        wait_gy(e, p)
        rows = [recv_y[e, pl.ds(p * s.block + y, s.kx, stride=s.deep), :] for y in range(s.deep)]
        return dot(txt3[...], tall3(jnp.concatenate(rows, axis=1)))

    def modes_x(e, p, parts):
        high, low = parts
        sent = dot(tx3[...], jnp.concatenate([high, high, low], axis=0))
        for y in range(s.deep):
            send_y[e, pl.ds(p * s.block + y, s.kx, stride=s.deep), :] = sent[:, y * 128 : (y + 1) * 128]
        piece_gy(e, p)

    def modes_sum(e, partial):
        i = SUMS[e]
        send_s[i] = jnp.broadcast_to(partial, (2, 128))
        exchange_heavy(lambda n: send_s.at[i], recv_s.at[i, me_heavy], ss.at[i], rs.at[i])

    def modes_y(e):
        sent = jnp.zeros((s.ky, NX * 128), f32)
        for p in range(PIECES):
            wait_gy(e, p)
            field = []
            for x in range(NX):
                at = [p * s.block + (d * NX + x) * s.deep for d in range(s.gy)]
                field.append(jnp.concatenate([recv_y[e, a : a + s.deep, :] for a in at], axis=0))
            sent = sent + dot(ty3[p], tall3(jnp.concatenate(field, axis=1)))
        for x in range(NX):
            send_z[e, pl.ds(x, s.ky, stride=NX), :] = sent[:, x * 128 : (x + 1) * 128]
        if e in SUMS:
            i = SUMS[e]
            wait(recv_s.at[i], rs.at[i])
            partial = jnp.sum(recv_s[i].reshape(2 * s.heavy, 128), axis=0, keepdims=True) * 0.5
            send_zs[i, :, 0:8, :] = send_z[e].reshape(s.light, 8, 128)
            send_zs[i, :, 8:16, :] = jnp.broadcast_to(partial[None], (s.light, 8, 128))
        unit_gz(e)

    def modes_z(e):
        wait_gz(e)
        summed = None
        if e in SUMS:
            i = SUMS[e]
            arrived = recv_zs[i, :, 0:8, :].reshape(8 * s.light, 128)
            summed = total(recv_zs[i, :, 8:9, :].reshape(s.light, 128))
        else:
            arrived = recv_z[e]
        coeffs = dot(tz3[...], tall3(arrived))
        pieces = []
        for j in range(2):
            at = 2 * j * s.kz
            pieces.append(coeffs[at : at + s.kz] * low_half + coeffs[at + s.kz : at + 2 * s.kz] * high_half)
        values = jnp.concatenate(pieces, axis=0)
        return values + pltpu.roll(values, 64, 1), summed

    def mix_forward(values):
        high, low = split(values)
        low_lanes = lane < 64
        packed = jnp.where(low_lanes, high.astype(f32), low.astype(f32)).astype(jnp.bfloat16)
        mixed = jnp.zeros_like(values)
        mixed = jnp.zeros((s.modes, 256), f32)
        for t in range(16):
            mixed = mixed + dot(packed, expand[t]) * w2[:, :, t * 256 : (t + 1) * 256].reshape(s.modes, 256)
        mixed = mixed[:, :128] + mixed[:, 128:]
        return mixed + pltpu.roll(mixed, 64, 1)

    def mix_adjoint(values):
        mixed = jnp.zeros((2 * s.modes, 128), f32)
        values = jnp.concatenate([values, values], axis=1)
        for t in range(16):
            high, low = split(values * w2[:, :, t * 256 : (t + 1) * 256].reshape(s.modes, 256))
            packed = jnp.concatenate([high, low], axis=0)
            mixed = mixed + lax.dot_general(packed, expand[t], NT, preferred_element_type=f32)
        return mixed[: s.modes] + mixed[s.modes :]

    def scalar_z(i, coeffs):
        pieces = []
        for j in range(2):
            for z in range(2):
                mask = (lax.rem(lax.div(lane, s.rows), 2) == z).astype(f32)
                pieces.append(coeffs[j * s.kz : (j + 1) * s.kz] * mask)
        sent = dot(tzt3[...], tall3(jnp.concatenate(pieces, axis=0)))
        row = lax.broadcasted_iota(jnp.int32, sent.shape, 0)
        send_pz[i] = jnp.where(lax.rem(row, NX) == lax.div(lane, 2 * s.rows), sent, 0.0)
        exchange_light(lambda n: send_pz.at[i, eight(n)], recv_pz.at[i, eight(me_light)], spz.at[i], rpz.at[i])

    def scalar_y(i):
        wait(recv_pz.at[i], rpz.at[i])
        arrived = recv_pz[i]
        for d in range(s.gy):
            summed = jnp.sum(arrived * ym[d], axis=0, keepdims=True)
            send_py[i, d] = jnp.broadcast_to(summed, (2, 128))
        exchange_heavy(
            lambda n: send_py.at[i, lax.div(n, NX)], recv_py.at[i, me_heavy], spy.at[i], rpy.at[i]
        )

    def scalar_x(i):
        wait(recv_py.at[i], rpy.at[i])
        columns = recv_py[i].reshape(2 * s.heavy, 128).T
        plane[...] = jnp.dot(columns, txk[...], precision=HIGHEST, preferred_element_type=f32)
        return plane[pl.ds(pl.multiple_of(at_x * 2 * s.rows, 2 * s.rows), 2 * s.rows), :]

    def lines(x):
        return jnp.concatenate([x[:, y * 128 : (y + 1) * 128] for y in range(s.deep)], axis=0)

    def across(x):
        return jnp.concatenate([x[y * 128 : (y + 1) * 128] for y in range(s.deep)], axis=1)

    def mat(m, parts):
        high, low = lines(parts[0]), lines(parts[1])
        return across(dot(jnp.concatenate([high, high, low], axis=1), mats3[m]))

    def fold(x):
        x = jnp.sum(x, axis=0, keepdims=True)
        return sum(x[:, y * 128 : (y + 1) * 128] for y in range(s.deep))

    def local_rows(i, p, parts):
        high, low = lines(parts[0]), lines(parts[1])
        rows = lax.dot_general(mats3[4, 0:16, :], high, NT, preferred_element_type=f32)
        rows = rows + lax.dot_general(mats3[4, 128:144, :], high, NT, preferred_element_type=f32)
        rows = rows + lax.dot_general(mats3[4, 0:16, :], low, NT, preferred_element_type=f32)
        for y in range(s.deep):
            lb[i, p * s.deep + y : p * s.deep + y + 1, :] = rows[0:1, y * 128 : (y + 1) * 128]
            at = s.rows + p * s.deep + y
            lb[i, at : at + 1, :] = rows[1:2, y * 128 : (y + 1) * 128]

    wide_row = lambda x: jnp.concatenate([x] * s.deep, axis=1)
    lift_wide, one_wide, two_wide, read_wide = map(wide_row, (lift_row, bias_one, bias_two, read_row))
    empty = jnp.zeros((1, 128), f32)

    values = modes_kappa * gain_mix
    cells_z(B0K, jnp.concatenate([values[0:8] + bias_mix, values[8:]], axis=0))
    cells_z(B0R, modes_rhs * gain_mix)
    ready(tyt3)
    cells_y(B0K)
    cells_y(B0R)
    for p in range(PIECES):
        value, slope = gelu_parts(cells_x(B0K, p) + lift_wide * kb[p] + one_wide)
        act[p] = value
        slope_one[p] = slope
        modes_x(C0A, p, split(value))
    for p in range(PIECES):
        value = slope_one[p] * (cells_x(B0R, p) + lift_wide * rb[p])
        tan[p] = value
        modes_x(C0T, p, split(value))
    ready(ty3)
    modes_y(C0A)
    modes_y(C0T)
    wait(w2, rw.at[1])
    values, _ = modes_z(C0A)
    cells_z(D0A, mix_forward(values))
    values, _ = modes_z(C0T)
    cells_z(D0T, mix_forward(values))
    cells_y(D0A)
    cells_y(D0T)
    for p in range(PIECES):
        _, slope = gelu_parts(cells_x(D0A, p) + mat(mix_two, split(act[p])) + two_wide)
        slope_two[p] = slope
    norms = empty
    for p in range(PIECES):
        slope = slope_two[p]
        tangent = slope * (cells_x(D0T, p) + mat(mix_two, split(tan[p])))
        predicted = mat(read_mat, split(tangent))
        pred0[p] = predicted
        weighted = wb[p] * predicted
        value = slope * (read_wide * weighted)
        back[p] = value
        modes_x(E0, p, split(value))
        norms = norms + fold(weighted * predicted)
    modes_sum(E0, norms)
    modes_y(E0)
    values, curvature = modes_z(E0)
    curvature = curvature * (1.0 / 64.0) + DAMPING * norm_zero
    step_zero = norm_zero / curvature
    cells_z(F0, mix_adjoint(values))
    cells_y(F0)
    for p in range(PIECES):
        value = slope_one[p] * (cells_x(F0, p) + mat(mix_back, split(back[p])))
        act[p] = value
        modes_x(G0, p, split(value))
    for p in range(PIECES):
        parts = split(act[p])
        local_rows(0, p, parts)
        qb[p] = rb[p] * (1.0 - DAMPING * step_zero) - step_zero * mat(lift_mat, parts)
    modes_y(G0)
    values, _ = modes_z(G0)

    coeffs_zero = jnp.sum(values * gain_mix * low_half, axis=1, keepdims=True)
    image = coeffs_zero + jnp.sum(values * lift_row * low_half, axis=1, keepdims=True) + DAMPING * modes_rhs
    modes_res = modes_rhs - step_zero * image
    cells_z(B1, modes_res * gain_mix - (step_zero * coeffs_zero) * lift_row)
    scalar_z(0, coeffs_zero)
    cells_y(B1)
    ready(ym)
    scalar_y(0)
    for p in range(PIECES):
        value = slope_one[p] * (cells_x(B1, p) + lift_wide * qb[p])
        tan[p] = value
        modes_x(C1, p, split(value))
    right = rhs[...]
    applied_zero = scalar_x(0) + lb[0] + DAMPING * right
    residual = right - step_zero * applied_zero
    modes_sum(C1, jnp.sum(residual * residual, axis=0, keepdims=True))
    modes_y(C1)
    values, norm_one = modes_z(C1)
    cells_z(D1, mix_forward(values))
    ratio = norm_one / norm_zero
    direction = residual + ratio * right
    cells_y(D1)
    norms = empty
    for p in range(PIECES):
        slope = slope_two[p]
        tangent = slope * (cells_x(D1, p) + mat(mix_two, split(tan[p])))
        predicted = mat(read_mat, split(tangent))
        value = slope * (read_wide * (wb[p] * predicted))
        back[p] = value
        modes_x(E1, p, split(value))
        moved = predicted + ratio * pred0[p]
        norms = norms + fold(wb[p] * moved * moved)
    norms = norms * (1.0 / 64.0) + DAMPING * jnp.sum(direction * direction, axis=0, keepdims=True)
    modes_sum(E1, norms)
    modes_y(E1)
    values, curvature = modes_z(E1)
    step_one = norm_one / curvature
    cells_z(F1, mix_adjoint(values))
    cells_y(F1)
    for p in range(PIECES):
        value = slope_one[p] * (cells_x(F1, p) + mat(mix_back, split(back[p])))
        act[p] = value
        modes_x(G1, p, split(value))
    for p in range(PIECES):
        local_rows(1, p, split(act[p]))
    modes_y(G1)
    values, _ = modes_z(G1)
    scalar_z(1, jnp.sum(values * gain_mix * low_half, axis=1, keepdims=True))
    scalar_y(1)
    applied = scalar_x(1) + lb[1] + DAMPING * residual + ratio * applied_zero
    out[0] = step_zero * right + step_one * direction
    out[1] = residual - step_one * applied

    for e in range(UNITS):
        wait(send_y.at[e, pl.ds(0, s.rows * (s.heavy - 1))], sy.at[e])
        if e in SUMS:
            wait(send_zs.at[SUMS[e], pl.ds(0, s.light - 1)], sz.at[e])
        else:
            wait(send_z.at[e, pl.ds(0, 8 * (s.light - 1))], sz.at[e])
    for i in range(3):
        wait(recv_s.at[i, pl.ds(0, s.heavy - 1)], ss.at[i])
    wait(send_a.at[pl.ds(0, s.heavy - 1)], sa.at[0])
    wait(recv_az.at[pl.ds(0, 8 * (s.light - 1))], sa.at[1])
    for i in range(2):
        wait(send_pz.at[i, pl.ds(0, 8 * (s.light - 1))], spz.at[i])
        wait(recv_py.at[i, pl.ds(0, s.heavy - 1)], spy.at[i])
    left(lambda j: gain_own.at[j], sw.at[0])
    left(lambda j: w2_in.at[j], sw.at[1])


def local(
    s,
    log_kappa,
    misfit_weight,
    right_side,
    lift_gain,
    lift_bias,
    spec_one,
    spec_two,
    local_one,
    local_two,
    bias_one,
    bias_two,
    readout,
):
    shape = log_kappa.shape
    rows = lambda x: x.reshape(2 * s.rows, s.line)
    row = lambda x: x.reshape(1, 64)
    tables = [jnp.asarray(t) for t in tables_of(s)]
    tx, txk, tx3, txt3, ty3, tyt3, tz3, tzt3, tza, ma, ym, expand, twice = tables
    near = [
        rows(log_kappa), rows(misfit_weight), rows(right_side),
        row(lift_gain), row(lift_bias), row(bias_one), row(bias_two), row(readout),
        local_one, local_two, tx, txk, tx3, txt3, tz3, tzt3, twice,
    ]
    far = [spec_one.reshape(s.modes, 4096), spec_two.reshape(2, s.kz, 4096), ty3, tyt3, tza, ma, ym, expand]
    f32, bf16 = jnp.float32, jnp.bfloat16
    vmem = lambda *dims: pltpu.VMEM(dims, f32)
    half = s.kx * s.rows
    cell = (PIECES, 128, 128 * s.deep)
    scratch = [
        vmem(UNITS, half, 128), vmem(UNITS, half, 128),
        vmem(UNITS, 8 * s.light, 128), vmem(UNITS, 8 * s.light, 128),
        vmem(3, s.light, 16, 128), vmem(3, s.light, 16, 128),
        vmem(3, 2, 128), vmem(3, s.heavy, 2, 128),
        vmem(s.heavy, 2, 128), vmem(s.heavy, 2, 128),
        vmem(8, 128), vmem(8 * s.light, 128),
        vmem(2, 8 * s.light, 128), vmem(2, 8 * s.light, 128),
        vmem(2, s.gy, 2, 128), vmem(2, s.heavy, 2, 128),
        pltpu.VMEM((5, 384, 128), bf16),
    ] + [vmem(*cell) for _ in range(10)] + [vmem(2, 2 * s.rows, 128), vmem(8, 64), vmem(128, 128)]
    scratch += [vmem(2, s.kz, 128), vmem(2, s.kz, 128)]
    scratch += [pltpu.VMEM(x.shape, x.dtype) for x in far]
    counts = [(UNITS,), (UNITS, PIECES), (UNITS,), (UNITS,), (3,), (3,), (2,), (2,), (2,), (2,), (2,), (2,), (2,), (2,), (len(far),)]
    scratch += [pltpu.SemaphoreType.DMA(n) for n in counts]
    result = pl.pallas_call(
        functools.partial(kernel, s),
        out_shape=jax.ShapeDtypeStruct((2, 2 * s.rows, s.line), f32),
        in_specs=[pl.BlockSpec(memory_space=pltpu.VMEM)] * len(near) + [pl.BlockSpec(memory_space=pl.ANY)] * len(far),
        out_specs=pl.BlockSpec(memory_space=pltpu.VMEM),
        scratch_shapes=scratch,
        compiler_params=pltpu.CompilerParams(
            collective_id=0, has_side_effects=True, vmem_limit_bytes=60 * 1024 * 1024
        ),
        name="two_steps",
    )(*near, *far)
    return tuple(result[i].reshape(shape) for i in range(2))


def solution(mesh, kx=KX, ky=KY, kz=KZ, rows=16, line=128):
    s = Sizes(mesh.shape["gz"], mesh.shape["gy"], rows, line, kx, ky, kz)
    field = P("gz", "gy", None)
    weights = P("gz", "gy", None, None)
    return jax.shard_map(
        functools.partial(local, s),
        mesh=mesh,
        in_specs=(field, field, field, P(), P(), weights, weights, P(), P(), P(), P(), P()),
        out_specs=(field, field),
        check_vma=False,
    )
```
